32 devices in a mesh: template: 4 (over y, core), fsdp: 4 (over z), dp: 2 (over x).
Axes of the slice: x: 2, y: 2, z: 4, core: 2. Of those that a mesh axis runs over, the one named last changes fastest.
Arguments:
- hidden: bfloat16 [4, 1024, 8192], P('template', ('fsdp', 'dp')), may hold values from -6 to 6
- target: bfloat16 [4, 1024, 512], P('template', ('fsdp', 'dp')), may hold values from -6 to 6
- weight: bfloat16 [4, 8192, 512], P('template', 'fsdp'), may hold values from -6 to 6
- gain: bfloat16 [4, 8192], P('template', 'fsdp'), may hold values from 0.099609375 to 1.8984375
Outputs:
- merged_weight: float32 [8192, 512], P(('fsdp', 'dp'))
- merged_gain: float32 [8192], P(('fsdp', 'dp'))
The draws below stay inside these ranges and needn't reach their ends.
All inputs are finite; a program needn't handle non-finite values.
Results may differ from the reference program's by a relative error of at most 0.0018.
Values may be sent and summed in bfloat16 or wider, within the bound.
A program may use at most 64 MiB of HBM per device.

```python
import math
import jax
import jax.numpy as jnp
from jax import lax

D = 8192
HD = 512
TEMPLATES = 4
TOKENS = 1024


def spiked(array, own_key, source, target, blocks, factor):
    owner, partner = [(jnp.arange(array.shape[axis_at]) // (array.shape[axis_at] // blocks)).reshape([-1 if axis == axis_at else 1 for axis in range(array.ndim)]) for axis_at in (source, target)]
    chosen = jax.random.permutation(own_key, blocks)[partner]
    strong = (owner == chosen) | (owner == (partner + blocks // 2) % blocks)
    return jnp.where(strong, factor * array, array)


def levels(key, dims, split, smallest, high):
    level = 1.0
    for position, blocks in split:
        draws = jax.random.uniform(jax.random.fold_in(jax.random.fold_in(key, 6), position), (blocks,), jnp.float32, smallest / len(split), high / len(split))
        level = level * jnp.repeat(jnp.exp(draws), dims[position] // blocks).reshape((-1,) + (1,) * (len(dims) - 1 - position))
    return level


def gaussian(own_key, extent, deviation, reach, cuts=(), kind=jnp.bfloat16):
    entries = deviation * jax.random.normal(own_key, extent, jnp.float32)
    if cuts:
        entries = entries * levels(own_key, extent, cuts, -0.22, 0.18)
    return jnp.clip(entries, -reach, reach).astype(kind)


def bell_draw_with(rng, shape, width, reach, cuts, heavy, kind=jnp.bfloat16):
    result = width * jax.random.normal(rng, shape, jnp.float32)
    if cuts:
        result = result * levels(rng, shape, cuts, -0.22, 0.18)
    return jnp.clip(spiked(result, jax.random.fold_in(rng, 3), *heavy), -reach, reach).astype(kind)


def setup_inputs(seed: int = 0) -> dict:
    key_list = jax.random.split(jax.random.key(seed), 5)
    hidden = bell_draw_with(key_list[0], (TEMPLATES, TOKENS, D), 1.0, 6.0, ((0, 4), (1, 8)), (1, 2, 8, 2.0))
    target = gaussian(key_list[1], (TEMPLATES, TOKENS, HD), 1.0, 6.0, ((0, 4), (1, 8)))
    weight = gaussian(key_list[2], (TEMPLATES, D, HD), 1.0, 6.0, ((0, 4), (1, 4)))
    gain = jnp.clip(1.0 + 0.18 * jax.random.normal(key_list[3], (TEMPLATES, D), jnp.float32), 0.099609375, 1.8984375).astype(jnp.bfloat16)
    return dict(hidden=hidden, target=target, weight=weight, gain=gain)


def reference(hidden, target, weight, gain):
    scale = 1.0 / math.sqrt(D)

    def one_model(carry, index):
        num, den, gnum, gden = carry
        hidden_state = hidden[index].astype(jnp.float32)
        merge_quotient = lax.rsqrt(lax.optimization_barrier(jnp.mean(hidden_state * hidden_state, axis=1, keepdims=True)) + 1e-05)
        normalized_activation = hidden_state * merge_quotient
        gain_vector = gain[index].astype(jnp.float32)
        normalized_input = (normalized_activation * gain_vector[None, :]).astype(jnp.bfloat16)
        w = weight[index]
        values = jnp.dot(normalized_input, w, preferred_element_type=jnp.float32) * scale
        delta = (values - target[index].astype(jnp.float32)).astype(jnp.bfloat16)
        sq_normed = jnp.square(normalized_input.astype(jnp.float32)).astype(jnp.bfloat16)
        sq_delta = jnp.square(delta.astype(jnp.float32)).astype(jnp.bfloat16)
        fisher = jnp.dot(sq_normed.T, sq_delta, preferred_element_type=jnp.float32)
        backward_pass = jnp.dot(delta, w.T, preferred_element_type=jnp.float32) * scale
        gain_information_sum = lax.optimization_barrier(jnp.sum(jnp.square(backward_pass * normalized_activation), axis=0))
        wf = w.astype(jnp.float32)
        return ((num + fisher * wf, den + fisher, gnum + gain_information_sum * gain_vector, gden + gain_information_sum), None)
    start = (jnp.zeros((D, HD), jnp.float32), jnp.zeros((D, HD), jnp.float32), jnp.zeros((D,), jnp.float32), jnp.zeros((D,), jnp.float32))
    totals, unused = lax.scan(one_model, start, jnp.arange(TEMPLATES, dtype=jnp.int32))
    num, den, gnum, gden = totals
    return (num / den, gnum / gden)
```

```python
import functools
import math

import jax
import jax.numpy as jnp
from jax import lax
from jax.experimental import pallas as pl
from jax.experimental.pallas import tpu as pltpu
from jax.sharding import PartitionSpec as P

F32 = jnp.float32
BF16 = jnp.bfloat16
MESH = pl.DeviceIdType.MESH


def flip(a, k):
    b = 1
    while b <= k:
        if k & b:
            a = a + b - 2 * b * ((a // b) % 2)
        b *= 2
    return a


def far_first(n):
    return list(range(n // 2, n)) + list(range(1, n // 2))


def kernel(T, Z, X, h_ref, t_ref, w_ref, g_ref, o_ref, og_ref,
           recv, xbuf, rmine, rz, rx, rcol, ps, rs, dall, sqt, fsend, frecv,
           f1send, f1recv, wq, gbuf,
           h_ss, h_rs, r_ss, r_rs, x_ss, x_rs, rx_ss, rx_rs, p_ss, p_rs,
           d_ss, d_rs, e_ss, e_rs, w_ss, w_rs, f_ss, f_rs, g_ss, g_rs, o_ss, o_rs):
    m, z, x = (lax.axis_index(a) for a in ("template", "fsdp", "dp"))
    tb, D = h_ref.shape
    FS, H = w_ref.shape
    mine = FS // X
    Q = mine // T
    scale = 1.0 / math.sqrt(D)
    pending = []

    def zdev(k):
        return (m, flip(z, k), x)

    def xdev(k):
        return (m, z, flip(x, k))

    def tdev(k):
        return (flip(m, k), z, x)

    def send(src, dst, ss, rs_, dev):
        c = pltpu.make_async_remote_copy(src_ref=src, dst_ref=dst, send_sem=ss, recv_sem=rs_,
                                         device_id=dev, device_id_type=MESH)
        c.start()
        pending.append(c)

    def arrived(dst, sem):
        pltpu.make_async_copy(dst, dst, sem).wait()

    def rows(s):
        return pl.ds(s * tb, tb)

    def cols(a, width):
        return pl.ds(pl.multiple_of(a * width, width), width)

    peers = ([zdev(k) for k in range(1, Z)] + [xdev(k) for k in range(1, X)]
             + [tdev(k) for k in range(1, T)])
    barrier = pltpu.get_barrier_semaphore()
    for dev in peers:
        pl.semaphore_signal(barrier, inc=1, device_id=dev, device_id_type=MESH)
    pl.semaphore_wait(barrier, len(peers))

    for k in far_first(Z):
        send(h_ref.at[:, cols(flip(z, k), FS)], recv.at[k], h_ss.at[k], h_rs.at[k], zdev(k))
    for j in range(1, X):
        send(h_ref.at[:, cols(z * X + flip(x, j), mine)], xbuf.at[rows(j * Z)],
             x_ss.at[j * Z], x_rs.at[j * Z], xdev(j))
    for k in range(1, T):
        send(w_ref.at[cols(x * T + flip(m, k), Q)], wq.at[k], w_ss.at[k], w_rs.at[k], tdev(k))

    step = min(512, D)

    def add_squares(i, acc):
        c = h_ref[:, cols(i, step)].astype(F32)
        c = c * c
        for a in range(0, step, 128):
            acc = acc + c[:, a:a + 128]
        return acc

    acc = lax.fori_loop(0, D // step, add_squares, jnp.zeros((tb, 128), F32))
    ratio = lax.rsqrt(jnp.sum(acc, axis=1, keepdims=True) / D + 1e-05)
    full = jnp.broadcast_to(ratio, (tb, 128))
    rcol[rows(0), :] = full
    rmine[...] = full.T[0:8, :]
    for k in far_first(Z):
        send(rmine, rz.at[k], r_ss.at[k], r_rs.at[k], zdev(k))
    for j in range(1, X):
        send(rmine, rx.at[j * Z], rx_ss.at[j * Z], rx_rs.at[j * Z], xdev(j))

    def column(row_ref):
        return jnp.broadcast_to(row_ref[0:1, :], (128, 128)).T

    wstep = min(512, FS)

    def partial(block, first, slot):
        r = rcol[rows(slot), 0:1]

        def body(i, total):
            here = cols(i, wstep)
            there = pl.ds(pl.multiple_of(first + i * wstep, wstep), wstep)
            c = (block[:, there].astype(F32) * r * g_ref[:, here].astype(F32)).astype(BF16)
            return total + jnp.dot(c, w_ref[here, :], preferred_element_type=F32)

        return lax.fori_loop(0, FS // wstep, body, jnp.zeros((tb, H), F32))

    own = partial(h_ref, z * FS, 0)
    order = list(range(1, Z))
    for k in order:
        arrived(rz.at[k], r_rs.at[k])
        arrived(recv.at[k], h_rs.at[k])
        for j in range(1, X):
            send(recv.at[k, :, cols(flip(x, j), mine)], xbuf.at[rows(j * Z + k)],
                 x_ss.at[j * Z + k], x_rs.at[j * Z + k], xdev(j))
            send(rz.at[k], rx.at[j * Z + k], rx_ss.at[j * Z + k], rx_rs.at[j * Z + k], xdev(j))
        rcol[rows(k), :] = column(rz.at[k])
        ps[k] = partial(recv.at[k], 0, k).astype(BF16)
        send(ps.at[k], rs.at[k], p_ss.at[k], p_rs.at[k], zdev(k))

    gain = g_ref[:, cols(x, mine)].astype(F32)
    fstep = min(256, mine)

    def square_slot(slot):
        r = rcol[rows(slot), 0:1]

        def body(i, _):
            here = cols(i, fstep)
            g = g_ref[:, pl.ds(pl.multiple_of(x * mine + i * fstep, fstep), fstep)].astype(F32)
            n = (xbuf[rows(slot), here].astype(F32) * r * g).astype(BF16).astype(F32)
            sqt[here, slot * tb:(slot + 1) * tb] = (n * n).T.astype(BF16)
            return 0

        lax.fori_loop(0, mine // fstep, body, 0)

    xbuf[rows(0), :] = h_ref[:, cols(z * X + x, mine)]
    square_slot(0)
    for k in order:
        xbuf[rows(k), :] = recv[k, :, cols(x, mine)]
        square_slot(k)

    values = own
    for k in order:
        arrived(rs.at[k], p_rs.at[k])
        values = values + rs[k].astype(F32)
    dall[rows(0), :] = (values * scale - t_ref[...].astype(F32)).astype(BF16)
    for k in far_first(Z):
        send(dall.at[rows(0)], dall.at[rows(k)], d_ss.at[k], d_rs.at[k], zdev(k))
    for j in range(1, X):
        send(dall.at[rows(0)], dall.at[rows(j * Z)], e_ss.at[j * Z], e_rs.at[j * Z], xdev(j))
    for j in range(1, X):
        for k in range(Z):
            s = j * Z + k
            arrived(rx.at[s], rx_rs.at[s])
            arrived(xbuf.at[rows(s)], x_rs.at[s])
            rcol[rows(s), :] = column(rx.at[s])
            square_slot(s)
    for k in order:
        arrived(dall.at[rows(k)], d_rs.at[k])
        for j in range(1, X):
            s = j * Z + k
            send(dall.at[rows(k)], dall.at[rows(s)], e_ss.at[s], e_rs.at[s], xdev(j))
    for j in range(1, X):
        for k in range(Z):
            s = j * Z + k
            arrived(dall.at[rows(s)], e_rs.at[s])

    tokens = X * Z * tb
    tstep = min(512, tokens)

    def fisher(q):
        def body(i, total):
            here = cols(i, tstep)
            d = dall[here, :].astype(F32)
            return total + jnp.dot(sqt[cols(q, Q), here], (d * d).astype(BF16),
                                   preferred_element_type=F32)

        return lax.fori_loop(0, tokens // tstep, body, jnp.zeros((Q, H), F32))

    for k in far_first(T):
        if k == 1:
            f1send[...] = fisher(flip(m, k))
            send(f1send, f1recv, f_ss.at[k], f_rs.at[k], tdev(k))
        else:
            fsend[k] = fisher(flip(m, k)).astype(BF16)
            send(fsend.at[k], frecv.at[k], f_ss.at[k], f_rs.at[k], tdev(k))
    den = fisher(m)
    num = den * w_ref[cols(x * T + m, Q), :].astype(F32)

    def back_slot(s, total):
        here = cols(s, tb)
        b = lax.dot_general(dall[here, :], w_ref[cols(x, mine), :], (((1,), (1,)), ((), ())),
                            preferred_element_type=F32) * scale
        b = b * (xbuf[here, :].astype(F32) * rcol[here, 0:1])
        return total + jnp.sum(b * b, axis=0, keepdims=True)

    gfish = lax.fori_loop(0, X * Z, back_slot, jnp.zeros((1, mine), F32))
    gbuf[0, 0:1, :] = gfish * gain
    gbuf[0, 1:2, :] = gfish
    gbuf[0, 2:8, :] = jnp.zeros((6, mine), F32)
    for k in range(1, T):
        send(gbuf.at[0], gbuf.at[k], g_ss.at[k], g_rs.at[k], tdev(k))

    for k in range(1, T):
        arrived(wq.at[k], w_rs.at[k])
        if k == 1:
            arrived(f1recv, f_rs.at[k])
            f = f1recv[...]
        else:
            arrived(frecv.at[k], f_rs.at[k])
            f = frecv[k].astype(F32)
        den = den + f
        num = num + f * wq[k].astype(F32)
    o_ref[cols(m, Q), :] = num / den
    held = [0]
    b = T // 2
    while b:
        for j in held:
            block = o_ref.at[cols(flip(m, j), Q)]
            send(block, block, o_ss.at[j ^ b], o_rs.at[j ^ b], tdev(b))
        for j in held:
            arrived(o_ref.at[cols(flip(m, j ^ b), Q)], o_rs.at[j ^ b])
        held = held + [j ^ b for j in held]
        b //= 2

    for k in range(1, T):
        arrived(gbuf.at[k], g_rs.at[k])
    sums = [gbuf[k] for k in range(T)]
    while len(sums) > 1:
        sums = [sums[i] + sums[i + 1] for i in range(0, len(sums), 2)]
    og_ref[...] = sums[0][0:1, :] / sums[0][1:2, :]
    for c in pending:
        c.wait_send()


def body(T, Z, X, hidden, target, weight, gain):
    _, tb, D = hidden.shape
    _, FS, H = weight.shape
    mine = FS // X
    Q = mine // T
    S = X * Z
    dma = lambda n: pltpu.SemaphoreType.DMA((n,))
    vmem = pltpu.VMEM
    flops = 2 * S * tb * mine * H * 3
    merged, merged_gain = pl.pallas_call(
        functools.partial(kernel, T, Z, X),
        out_shape=(jax.ShapeDtypeStruct((mine, H), F32), jax.ShapeDtypeStruct((1, mine), F32)),
        in_specs=[pl.BlockSpec(memory_space=pltpu.VMEM)] * 4,
        out_specs=[pl.BlockSpec(memory_space=pltpu.VMEM)] * 2,
        scratch_shapes=[
            vmem((Z, tb, FS), BF16),
            vmem((S * tb, mine), BF16),
            vmem((8, 128), F32),
            vmem((Z, 8, 128), F32),
            vmem((S, 8, 128), F32),
            vmem((S * tb, 128), F32),
            vmem((Z, tb, H), BF16),
            vmem((Z, tb, H), BF16),
            vmem((S * tb, H), BF16),
            vmem((mine, S * tb), BF16),
            vmem((T, Q, H), BF16),
            vmem((T, Q, H), BF16),
            vmem((Q, H), F32),
            vmem((Q, H), F32),
            vmem((T, Q, H), BF16),
            vmem((T, 8, mine), F32),
            dma(Z), dma(Z), dma(Z), dma(Z), dma(S), dma(S), dma(S), dma(S), dma(Z), dma(Z),
            dma(Z), dma(Z), dma(S), dma(S), dma(T), dma(T), dma(T), dma(T), dma(T), dma(T),
            dma(T), dma(T),
        ],
        cost_estimate=pl.CostEstimate(flops=flops, bytes_accessed=8 << 20, transcendentals=0),
        compiler_params=pltpu.CompilerParams(
            collective_id=0, has_side_effects=True, vmem_limit_bytes=56 << 20),
    )(hidden[0], target[0], weight[0], gain)
    return merged, merged_gain[0]


def solution(mesh):
    T, Z, X = (mesh.shape[a] for a in ("template", "fsdp", "dp"))
    in_specs = (
        P("template", ("fsdp", "dp"), None),
        P("template", ("fsdp", "dp"), None),
        P("template", "fsdp", None),
        P("template", "fsdp"),
    )
    out_specs = (P(("fsdp", "dp"), None), P(("fsdp", "dp")))
    return jax.shard_map(functools.partial(body, T, Z, X), mesh=mesh, in_specs=in_specs,
                         out_specs=out_specs, check_vma=False)
```

```python
import functools
import math

import jax
import jax.numpy as jnp
from jax import lax
from jax.experimental import pallas as pl
from jax.experimental.pallas import tpu as pltpu
from jax.sharding import PartitionSpec as P

F32 = jnp.float32
BF16 = jnp.bfloat16
MESH = pl.DeviceIdType.MESH


def flip(a, k):
    b = 1
    while b <= k:
        if k & b:
            a = a + b - 2 * b * ((a // b) % 2)
        b *= 2
    return a


def far_first(n):
    return list(range(n // 2, n)) + list(range(1, n // 2))


def backward_bits(p, n):
    k, b = 0, n // 2
    while b:
        if p & 1:
            k += b
        p //= 2
        b //= 2
    return k


def kernel(T, Z, X, C, U, h_ref, t_ref, w_ref, g_ref, o_ref, og_ref,
           recv, xbuf, rz, rx, rcol, pacc, ps, rs, dall, sqt, facc, fsend, frecv,
           f1send, f1recv, wq, gbuf,
           h_ss, h_rs, r_ss, r_rs, x_ss, x_rs, rx_ss, rx_rs, p_ss, p_rs,
           d_ss, d_rs, e_ss, e_rs, w_ss, w_rs, f_ss, f_rs, g_ss, g_rs, o_ss, o_rs):
    m, z, x = (lax.axis_index(a) for a in ("template", "fsdp", "dp"))
    tb, D = h_ref.shape
    FS, H = w_ref.shape
    mine = FS // X
    Q = mine // T
    QU = Q // U
    tc = tb // C
    ZR = Z * tc
    NR = X * ZR
    scale = 1.0 / math.sqrt(D)
    pending = []

    def zdev(k):
        return (m, flip(z, k), x)

    def xdev(k):
        return (m, z, flip(x, k))

    def tdev(k):
        return (flip(m, k), z, x)

    def send(src, dst, ss, rs_, dev):
        c = pltpu.make_async_remote_copy(src_ref=src, dst_ref=dst, send_sem=ss, recv_sem=rs_,
                                         device_id=dev, device_id_type=MESH)
        c.start()
        pending.append(c)

    def arrived(dst, sem):
        pltpu.make_async_copy(dst, dst, sem).wait()

    def cols(a, width):
        return pl.ds(pl.multiple_of(a * width, width), width)

    def at(first, n):
        return pl.ds(first, n)

    peers = ([zdev(k) for k in range(1, Z)] + [xdev(k) for k in range(1, X)]
             + [tdev(k) for k in range(1, T)])
    barrier = pltpu.get_barrier_semaphore()
    for dev in peers:
        pl.semaphore_signal(barrier, inc=1, device_id=dev, device_id_type=MESH)
    pl.semaphore_wait(barrier, len(peers))

    def send_hidden(c):
        for p in sorted(range(1, Z), key=lambda p: -(p & 1)):
            k = backward_bits(p, Z)
            send(h_ref.at[at(c * tc, tc), cols(flip(z, k), FS)], recv.at[at(c * ZR + p * tc, tc)],
                 h_ss.at[c * Z + p], h_rs.at[c * Z + p], zdev(k))

    send_hidden(0)

    step = min(512, D)

    def add_squares(i, acc):
        c = h_ref[:, cols(i, step)].astype(F32)
        c = c * c
        for a in range(0, step, 128):
            acc = acc + c[:, a:a + 128]
        return acc

    acc = lax.fori_loop(0, D // step, add_squares, jnp.zeros((tb, 128), F32))
    ratio = lax.rsqrt(jnp.sum(acc, axis=1, keepdims=True) / D + 1e-05)
    rz[0] = jnp.broadcast_to(ratio, (tb, 128)).T[0:8, :]
    for p in range(1, Z):
        k = backward_bits(p, Z)
        send(rz.at[0], rz.at[p], r_ss.at[p], r_rs.at[p], zdev(k))
    if C > 1:
        send_hidden(1)
    for k in range(1, T):
        send(w_ref.at[cols(x * T + flip(m, k), Q)], wq.at[k], w_ss.at[k], w_rs.at[k], tdev(k))

    def put_column(row_ref, j, p):
        col = jnp.broadcast_to(row_ref[0:1, :], (128, 128)).T
        for c in range(C):
            rcol[at((c * X + j) * ZR + p * tc, tc), :] = col[c * tc:(c + 1) * tc, :]

    wstep = min(512, FS)

    def partial(c):
        r = rcol[at(c * NR, ZR), 0:1]

        def body(i, total):
            here = cols(i, wstep)
            n = (recv[at(c * ZR, ZR), here].astype(F32) * r
                 * g_ref[:, here].astype(F32)).astype(BF16)
            return total + jnp.dot(n, w_ref[here, :], preferred_element_type=F32)

        pacc[...] = lax.fori_loop(0, FS // wstep, body, jnp.zeros((ZR, H), F32))

    fstep = min(256, mine)

    def squares(c, j):
        first = (c * X + j) * ZR
        r = rcol[at(first, ZR), 0:1]

        def body(i, _):
            here = cols(i, fstep)
            g = g_ref[:, pl.ds(pl.multiple_of(x * mine + i * fstep, fstep), fstep)].astype(F32)
            n = (xbuf[at(first, ZR), here].astype(F32) * r * g).astype(BF16).astype(F32)
            sqt[here, first:first + ZR] = (n * n).T.astype(BF16)
            return 0

        lax.fori_loop(0, mine // fstep, body, 0)

    def other_squares(c):
        for j in range(1, X):
            if c == 0:
                arrived(rx.at[j], rx_rs.at[j])
                for p in range(Z):
                    put_column(rx.at[j, p], j, p)
            arrived(xbuf.at[at((c * X + j) * ZR, ZR)], x_rs.at[c * X + j])
            squares(c, j)

    def residuals_here(c):
        for j in range(1, X):
            n = 0
            while n < Z:
                size = max(n, 1) * tc
                first = (c * X + j) * ZR + n * tc
                arrived(dall.at[at(first, size)], e_rs.at[(c * X + j) * Z + n])
                n = max(2 * n, 1)

    def forward(c, n):
        size = max(n, 1) * tc
        for j in range(1, X):
            send(dall.at[at(c * NR + n * tc, size)], dall.at[at((c * X + j) * ZR + n * tc, size)],
                 e_ss.at[(c * X + j) * Z + n], e_rs.at[(c * X + j) * Z + n], xdev(j))

    def fisher(c, first, size):
        d = dall[at(c * NR, NR), :].astype(F32)
        f = jnp.dot(sqt[pl.ds(first, size), c * NR:(c + 1) * NR], (d * d).astype(BF16),
                    preferred_element_type=F32)
        if c:
            f = f + facc[pl.ds(first, size), :]
        return f

    def add_fisher(c):
        size = min(256, mine)

        def body(i, _):
            first = pl.multiple_of(i * size, size)
            facc[pl.ds(first, size), :] = fisher(c, first, size)
            return 0

        lax.fori_loop(0, mine // size, body, 0)

    def back(c, total):
        def body(i, total):
            here = pl.ds(pl.multiple_of(c * NR + i * ZR, ZR), ZR)
            b = lax.dot_general(dall[here, :], w_ref[cols(x, mine), :], (((1,), (1,)), ((), ())),
                                preferred_element_type=F32) * scale
            b = b * (xbuf[here, :].astype(F32) * rcol[here, 0:1])
            return total + jnp.sum(b * b, axis=0, keepdims=True)

        return lax.fori_loop(0, X, body, total)

    gfish = jnp.zeros((1, mine), F32)
    for c in range(C):
        recv[at(c * ZR, tc), :] = h_ref[at(c * tc, tc), cols(z, FS)]
        if c == 0:
            put_column(rz.at[0], 0, 0)
            for p in range(1, Z):
                arrived(rz.at[p], r_rs.at[p])
                put_column(rz.at[p], 0, p)
            for j in range(1, X):
                send(rz, rx.at[j], rx_ss.at[j], rx_rs.at[j], xdev(j))
        for p in range(1, Z):
            arrived(recv.at[at(c * ZR + p * tc, tc)], h_rs.at[c * Z + p])
        if c + 2 < C:
            send_hidden(c + 2)
        for j in range(1, X):
            send(recv.at[at(c * ZR, ZR), cols(flip(x, j), mine)],
                 xbuf.at[at((c * X + j) * ZR, ZR)], x_ss.at[c * X + j], x_rs.at[c * X + j], xdev(j))
        partial(c)
        n, b = Z, 1
        while n > 1:
            half = n // 2
            size = half * tc
            there = at((c * Z + half) * tc, size)
            ps[there, :] = pacc[at(size, size), :].astype(BF16)
            send(ps.at[there], rs.at[there], p_ss.at[c * Z + half], p_rs.at[c * Z + half], zdev(b))
            if b == 1:
                xbuf[at(c * NR, ZR), :] = recv[at(c * ZR, ZR), cols(x, mine)]
                squares(c, 0)
            arrived(rs.at[there], p_rs.at[c * Z + half])
            pacc[at(0, size), :] += rs[there, :].astype(F32)
            n, b = half, b * 2
        dall[at(c * NR, tc), :] = (pacc[at(0, tc), :] * scale
                                   - t_ref[at(c * tc, tc), :].astype(F32)).astype(BF16)
        n, b = 1, Z // 2
        while n < Z:
            size = n * tc
            send(dall.at[at(c * NR, size)], dall.at[at(c * NR + size, size)],
                 d_ss.at[c * Z + n], d_rs.at[c * Z + n], zdev(b))
            if n == 1:
                forward(c, 0)
                if c:
                    residuals_here(c - 1)
                    add_fisher(c - 1)
                other_squares(c)
            arrived(dall.at[at(c * NR + size, size)], d_rs.at[c * Z + n])
            forward(c, n)
            n, b = 2 * n, b // 2
        if 0 < c < C - 1:
            gfish = back(c - 1, gfish)
    residuals_here(C - 1)

    for u in range(U):
        for k in far_first(T):
            f = fisher(C - 1, pl.multiple_of(flip(m, k) * Q + u * QU, QU), QU)
            i = k * U + u
            part = at(u * QU, QU)
            if k == 1:
                f1send[part, :] = f
                send(f1send.at[part], f1recv.at[part], f_ss.at[i], f_rs.at[i], tdev(k))
            else:
                fsend[k, part, :] = f.astype(BF16)
                send(fsend.at[k, part], frecv.at[k, part], f_ss.at[i], f_rs.at[i], tdev(k))
    for c in range(max(C - 2, 0), C):
        gfish = back(c, gfish)
    gbuf[0, 0:1, :] = gfish * g_ref[:, cols(x, mine)].astype(F32)
    gbuf[0, 1:2, :] = gfish
    gbuf[0, 2:8, :] = jnp.zeros((6, mine), F32)
    for k in range(1, T):
        send(gbuf.at[0], gbuf.at[k], g_ss.at[k], g_rs.at[k], tdev(k))

    def block(j, u):
        return o_ref.at[pl.ds(pl.multiple_of(flip(m, j) * Q + u * QU, QU), QU)]

    def share(j, b, u):
        i = (j ^ b) * U + u
        send(block(j, u), block(j, u), o_ss.at[i], o_rs.at[i], tdev(b))

    for u in range(U):
        first = pl.multiple_of(m * Q + u * QU, QU)
        part = at(u * QU, QU)
        den = fisher(C - 1, first, QU)
        num = den * w_ref[pl.ds(pl.multiple_of(x * mine + m * Q + u * QU, QU), QU), :].astype(F32)
        for k in range(1, T):
            if u == 0:
                arrived(wq.at[k], w_rs.at[k])
            i = k * U + u
            if k == 1:
                arrived(f1recv.at[part], f_rs.at[i])
                f = f1recv[part, :]
            else:
                arrived(frecv.at[k, part], f_rs.at[i])
                f = frecv[k, part, :].astype(F32)
            den = den + f
            num = num + f * wq[k, part, :].astype(F32)
        o_ref[pl.ds(first, QU), :] = num / den
        share(0, T // 2, u)
    held, b = [0], T // 2
    while b > 1:
        for u in range(U):
            for j in held:
                arrived(block(j ^ b, u), o_rs.at[(j ^ b) * U + u])
                share(j, b // 2, u)
                share(j ^ b, b // 2, u)
        held = held + [j ^ b for j in held]
        b //= 2

    for k in range(1, T):
        arrived(gbuf.at[k], g_rs.at[k])
    sums = [gbuf[k] for k in range(T)]
    while len(sums) > 1:
        sums = [sums[i] + sums[i + 1] for i in range(0, len(sums), 2)]
    og_ref[...] = sums[0][0:1, :] / sums[0][1:2, :]
    for u in range(U):
        for j in held:
            arrived(block(j ^ 1, u), o_rs.at[(j ^ 1) * U + u])
    for c in pending:
        c.wait_send()


def body(T, Z, X, hidden, target, weight, gain):
    _, tb, D = hidden.shape
    _, FS, H = weight.shape
    mine = FS // X
    Q = mine // T
    S = X * Z
    C = 4
    U = 2 if Q >= 64 else 1
    dma = lambda n: pltpu.SemaphoreType.DMA((n,))
    vmem = pltpu.VMEM
    flops = 2 * S * tb * mine * H * 3
    merged, merged_gain = pl.pallas_call(
        functools.partial(kernel, T, Z, X, C, U),
        out_shape=(jax.ShapeDtypeStruct((mine, H), F32), jax.ShapeDtypeStruct((1, mine), F32)),
        in_specs=[pl.BlockSpec(memory_space=pltpu.VMEM)] * 4,
        out_specs=[pl.BlockSpec(memory_space=pltpu.VMEM)] * 2,
        scratch_shapes=[
            vmem((Z * tb, FS), BF16),
            vmem((S * tb, mine), BF16),
            vmem((Z, 8, 128), F32),
            vmem((X, Z, 8, 128), F32),
            vmem((S * tb, 128), F32),
            vmem((Z * tb // C, H), F32),
            vmem((Z * tb, H), BF16),
            vmem((Z * tb, H), BF16),
            vmem((S * tb, H), BF16),
            vmem((mine, S * tb), BF16),
            vmem((mine, H), F32),
            vmem((T, Q, H), BF16),
            vmem((T, Q, H), BF16),
            vmem((Q, H), F32),
            vmem((Q, H), F32),
            vmem((T, Q, H), BF16),
            vmem((T, 8, mine), F32),
            dma(C * Z), dma(C * Z), dma(Z), dma(Z), dma(C * X), dma(C * X), dma(X), dma(X),
            dma(C * Z), dma(C * Z), dma(C * Z), dma(C * Z), dma(C * S), dma(C * S),
            dma(T), dma(T), dma(T * U), dma(T * U), dma(T), dma(T), dma(T * U), dma(T * U),
        ],
        cost_estimate=pl.CostEstimate(flops=flops, bytes_accessed=8 << 20, transcendentals=0),
        compiler_params=pltpu.CompilerParams(
            collective_id=0, has_side_effects=True, vmem_limit_bytes=56 << 20),
    )(hidden[0], target[0], weight[0], gain)
    return merged, merged_gain[0]


def solution(mesh):
    T, Z, X = (mesh.shape[a] for a in ("template", "fsdp", "dp"))
    in_specs = (
        P("template", ("fsdp", "dp"), None),
        P("template", ("fsdp", "dp"), None),
        P("template", "fsdp", None),
        P("template", "fsdp"),
    )
    out_specs = (P(("fsdp", "dp"), None), P(("fsdp", "dp")))
    return jax.shard_map(functools.partial(body, T, Z, X), mesh=mesh, in_specs=in_specs,
                         out_specs=out_specs, check_vma=False)
```

```python
import functools
import math

import jax
import jax.numpy as jnp
from jax import lax
from jax.experimental import pallas as pl
from jax.experimental.pallas import tpu as pltpu
from jax.sharding import PartitionSpec as P

F32 = jnp.float32
BF16 = jnp.bfloat16
MESH = pl.DeviceIdType.MESH


def flip(a, k):
    b = 1
    while b <= k:
        if k & b:
            a = a + b - 2 * b * ((a // b) % 2)
        b *= 2
    return a


def far_first(n):
    return list(range(n // 2, n)) + list(range(1, n // 2))


def kernel(T, Z, X, C, B, h_ref, t_ref, w_ref, g_ref, o_ref, og_ref,
           recv, xbuf, rz, rx, rcol, own, ps, rs, dall, sqt, fsend, frecv,
           f1send, f1recv, wq, gbuf,
           h_ss, h_rs, r_ss, r_rs, x_ss, x_rs, rx_ss, rx_rs, p_ss, p_rs,
           d_ss, d_rs, e_ss, e_rs, w_ss, w_rs, f_ss, f_rs, g_ss, g_rs, o_ss, o_rs):
    m, z, x = (lax.axis_index(a) for a in ("template", "fsdp", "dp"))
    tb, D = h_ref.shape
    FS, H = w_ref.shape
    mine = FS // X
    Q = mine // T
    tc = tb // C
    ZR = Z * tc
    HB = H // B
    tokens = C * X * ZR
    scale = 1.0 / math.sqrt(D)
    pending = []

    def zdev(k):
        return (m, flip(z, k), x)

    def xdev(k):
        return (m, z, flip(x, k))

    def tdev(k):
        return (flip(m, k), z, x)

    def send(src, dst, ss, rs_, dev):
        c = pltpu.make_async_remote_copy(src_ref=src, dst_ref=dst, send_sem=ss, recv_sem=rs_,
                                         device_id=dev, device_id_type=MESH)
        c.start()
        pending.append(c)

    def arrived(dst, sem):
        pltpu.make_async_copy(dst, dst, sem).wait()

    def cols(a, width):
        return pl.ds(pl.multiple_of(a * width, width), width)

    peers = ([zdev(k) for k in range(1, Z)] + [xdev(k) for k in range(1, X)]
             + [tdev(k) for k in range(1, T)])
    barrier = pltpu.get_barrier_semaphore()
    for dev in peers:
        pl.semaphore_signal(barrier, inc=1, device_id=dev, device_id_type=MESH)
    pl.semaphore_wait(barrier, len(peers))

    for c in range(C):
        for k in far_first(Z):
            send(h_ref.at[pl.ds(c * tc, tc), cols(flip(z, k), FS)], recv.at[c, k],
                 h_ss.at[c * Z + k], h_rs.at[c * Z + k], zdev(k))

    step = min(512, D)

    def add_squares(i, acc):
        c = h_ref[:, cols(i, step)].astype(F32)
        c = c * c
        for a in range(0, step, 128):
            acc = acc + c[:, a:a + 128]
        return acc

    acc = lax.fori_loop(0, D // step, add_squares, jnp.zeros((tb, 128), F32))
    ratio = lax.rsqrt(jnp.sum(acc, axis=1, keepdims=True) / D + 1e-05)
    rz[0] = jnp.broadcast_to(ratio, (tb, 128)).T[0:8, :]
    for k in far_first(Z):
        send(rz.at[0], rz.at[k], r_ss.at[k], r_rs.at[k], zdev(k))
    for k in range(1, T):
        send(w_ref.at[cols(x * T + flip(m, k), Q)], wq.at[k], w_ss.at[k], w_rs.at[k], tdev(k))

    def put_column(row_ref, j, k):
        col = jnp.broadcast_to(row_ref[0:1, :], (128, 128)).T
        for c in range(C):
            rcol[c, j, k] = col[c * tc:(c + 1) * tc, :]

    wstep = min(512, FS)

    def partial(c):
        r = rcol[c, 0].reshape(ZR, 128)[:, 0:1]

        def body(i, total):
            here = cols(i, wstep)
            n = (recv[c, :, :, here].reshape(ZR, wstep).astype(F32) * r
                 * g_ref[:, here].astype(F32)).astype(BF16)
            return total + jnp.dot(n, w_ref[here, :], preferred_element_type=F32)

        v = lax.fori_loop(0, FS // wstep, body, jnp.zeros((ZR, H), F32))
        own[pl.ds(c * tc, tc), :] = v[0:tc, :]
        for i in range(B):
            for k in range(1, Z):
                ps[i, k, pl.ds(c * tc, tc), :] = (
                    v[k * tc:(k + 1) * tc, i * HB:(i + 1) * HB].astype(BF16))

    fstep = min(256, mine)

    def squares(c, j):
        r = rcol[c, j].reshape(ZR, 128)[:, 0:1]
        first = (c * X + j) * ZR

        def body(i, _):
            here = cols(i, fstep)
            g = g_ref[:, pl.ds(pl.multiple_of(x * mine + i * fstep, fstep), fstep)].astype(F32)
            n = xbuf[c, j, :, :, here].reshape(ZR, fstep).astype(F32) * r * g
            n = n.astype(BF16).astype(F32)
            sqt[here, first:first + ZR] = (n * n).T.astype(BF16)
            return 0

        lax.fori_loop(0, mine // fstep, body, 0)

    def own_squares(c):
        xbuf[c, 0] = recv[c, :, :, cols(x, mine)]
        squares(c, 0)

    def other_squares(c):
        for j in range(1, X):
            if c == 0:
                arrived(rx.at[j], rx_rs.at[j])
                for k in range(Z):
                    put_column(rx.at[j, k], j, k)
            arrived(xbuf.at[c, j], x_rs.at[c * X + j])
            squares(c, j)

    for c in range(C):
        recv[c, 0] = h_ref[pl.ds(c * tc, tc), cols(z, FS)]
    put_column(rz.at[0], 0, 0)
    for k in range(1, Z):
        arrived(rz.at[k], r_rs.at[k])
        put_column(rz.at[k], 0, k)
    for j in range(1, X):
        send(rz, rx.at[j], rx_ss.at[j], rx_rs.at[j], xdev(j))
    for c in range(C):
        for k in far_first(Z):
            arrived(recv.at[c, k], h_rs.at[c * Z + k])
        for j in range(1, X):
            send(recv.at[c, :, :, cols(flip(x, j), mine)], xbuf.at[c, j],
                 x_ss.at[c * X + j], x_rs.at[c * X + j], xdev(j))
        partial(c)
        if c < C - 1:
            own_squares(c)
            if c:
                other_squares(c - 1)

    def give_partials(i):
        for k in far_first(Z):
            send(ps.at[i, k], rs.at[i, k], p_ss.at[i * Z + k], p_rs.at[i * Z + k], zdev(k))

    def residual(i):
        here = slice(i * HB, (i + 1) * HB)
        v = own[:, here]
        for k in range(1, Z):
            arrived(rs.at[i, k], p_rs.at[i * Z + k])
            v = v + rs[i, k].astype(F32)
        d = (v * scale - t_ref[:, here].astype(F32)).astype(BF16)
        dall[i, :, 0, 0] = d.reshape(C, tc, HB)
        for k in far_first(Z):
            send(dall.at[i, :, 0, 0], dall.at[i, :, 0, k], d_ss.at[i * Z + k], d_rs.at[i * Z + k],
                 zdev(k))
        forward(i, 0)

    def forward(i, k):
        for j in range(1, X):
            s = (i * X + j) * Z + k
            send(dall.at[i, :, 0, k], dall.at[i, :, j, k], e_ss.at[s], e_rs.at[s], xdev(j))

    def residuals_on(i):
        for k in far_first(Z):
            arrived(dall.at[i, :, 0, k], d_rs.at[i * Z + k])
            forward(i, k)

    def fisher_rows(i, q):
        d = dall[i].reshape(tokens, HB).astype(F32)
        return jnp.dot(sqt[cols(q, Q), :], (d * d).astype(BF16), preferred_element_type=F32)

    def fisher(i):
        for j in range(1, X):
            for k in range(Z):
                s = (i * X + j) * Z + k
                arrived(dall.at[i, :, j, k], e_rs.at[s])
        for k in far_first(T):
            f = fisher_rows(i, flip(m, k))
            if k == 1:
                f1send[i] = f
                send(f1send.at[i], f1recv.at[i], f_ss.at[i * T + k], f_rs.at[i * T + k], tdev(k))
            else:
                fsend[i, k] = f.astype(BF16)
                send(fsend.at[i, k], frecv.at[i, k], f_ss.at[i * T + k], f_rs.at[i * T + k],
                     tdev(k))

    def block(j, i):
        return o_ref.at[cols(flip(m, j), Q), pl.ds(i * HB, HB)]

    def share(j, b, i):
        s = i * T + (j ^ b)
        send(block(j, i), block(j, i), o_ss.at[s], o_rs.at[s], tdev(b))

    def merge(i):
        here = slice(i * HB, (i + 1) * HB)
        den = fisher_rows(i, m)
        num = den * w_ref[cols(x * T + m, Q), here].astype(F32)
        for k in range(1, T):
            if i == 0:
                arrived(wq.at[k], w_rs.at[k])
            if k == 1:
                arrived(f1recv.at[i], f_rs.at[i * T + k])
                f = f1recv[i]
            else:
                arrived(frecv.at[i, k], f_rs.at[i * T + k])
                f = frecv[i, k].astype(F32)
            den = den + f
            num = num + f * wq[k, :, here].astype(F32)
        o_ref[cols(m, Q), here] = num / den
        share(0, T // 2, i)

    def share_on(i):
        held, b = [0], T // 2
        while b > 1:
            for j in held:
                arrived(block(j ^ b, i), o_rs.at[i * T + (j ^ b)])
                share(j, b // 2, i)
                share(j ^ b, b // 2, i)
            held = held + [j ^ b for j in held]
            b //= 2

    def back(c, j, total):
        d = jnp.concatenate([dall[i, c, j].reshape(ZR, HB) for i in range(B)], axis=1)
        b = lax.dot_general(d, w_ref[cols(x, mine), :], (((1,), (1,)), ((), ())),
                            preferred_element_type=F32) * scale
        r = rcol[c, j].reshape(ZR, 128)[:, 0:1]
        b = b * (xbuf[c, j].reshape(ZR, mine).astype(F32) * r)
        return total + jnp.sum(b * b, axis=0, keepdims=True)

    give_partials(0)
    if B > 1:
        give_partials(1)
    own_squares(C - 1)
    if C > 1:
        other_squares(C - 2)
    for t in range(B + 4):
        if t < B:
            residual(t)
        if t + 2 < B:
            give_partials(t + 2)
        if t == 0:
            other_squares(C - 1)
        if 0 <= t - 1 < B:
            residuals_on(t - 1)
        if 0 <= t - 2 < B:
            fisher(t - 2)
        if 0 <= t - 3 < B:
            if t - 3 == B - 1:
                gfish = jnp.zeros((1, mine), F32)
                for c in range(C):
                    for j in range(X):
                        gfish = back(c, j, gfish)
                gbuf[0, 0:1, :] = gfish * g_ref[:, cols(x, mine)].astype(F32)
                gbuf[0, 1:2, :] = gfish
                gbuf[0, 2:8, :] = jnp.zeros((6, mine), F32)
                for k in range(1, T):
                    send(gbuf.at[0], gbuf.at[k], g_ss.at[k], g_rs.at[k], tdev(k))
            merge(t - 3)
        if 0 <= t - 4 < B:
            share_on(t - 4)

    for k in range(1, T):
        arrived(gbuf.at[k], g_rs.at[k])
    sums = [gbuf[k] for k in range(T)]
    while len(sums) > 1:
        sums = [sums[i] + sums[i + 1] for i in range(0, len(sums), 2)]
    og_ref[...] = sums[0][0:1, :] / sums[0][1:2, :]
    for i in range(B):
        for j in range(0, T, 2):
            arrived(block(j ^ 1, i), o_rs.at[i * T + (j ^ 1)])
    for c in pending:
        c.wait_send()


def body(T, Z, X, hidden, target, weight, gain):
    _, tb, D = hidden.shape
    _, FS, H = weight.shape
    mine = FS // X
    Q = mine // T
    S = X * Z
    C = 2
    B = H // 128
    tc = tb // C
    dma = lambda n: pltpu.SemaphoreType.DMA((n,))
    vmem = pltpu.VMEM
    flops = 2 * S * tb * mine * H * 3
    merged, merged_gain = pl.pallas_call(
        functools.partial(kernel, T, Z, X, C, B),
        out_shape=(jax.ShapeDtypeStruct((mine, H), F32), jax.ShapeDtypeStruct((1, mine), F32)),
        in_specs=[pl.BlockSpec(memory_space=pltpu.VMEM)] * 4,
        out_specs=[pl.BlockSpec(memory_space=pltpu.VMEM)] * 2,
        scratch_shapes=[
            vmem((C, Z, tc, FS), BF16),
            vmem((C, X, Z, tc, mine), BF16),
            vmem((Z, 8, 128), F32),
            vmem((X, Z, 8, 128), F32),
            vmem((C, X, Z, tc, 128), F32),
            vmem((tb, H), F32),
            vmem((B, Z, tb, H // B), BF16),
            vmem((B, Z, tb, H // B), BF16),
            vmem((B, C, X, Z, tc, H // B), BF16),
            vmem((mine, S * tb), BF16),
            vmem((B, T, Q, H // B), BF16),
            vmem((B, T, Q, H // B), BF16),
            vmem((B, Q, H // B), F32),
            vmem((B, Q, H // B), F32),
            vmem((T, Q, H), BF16),
            vmem((T, 8, mine), F32),
            dma(C * Z), dma(C * Z), dma(Z), dma(Z), dma(C * X), dma(C * X), dma(X), dma(X),
            dma(B * Z), dma(B * Z), dma(B * Z), dma(B * Z), dma(B * S), dma(B * S),
            dma(T), dma(T), dma(B * T), dma(B * T), dma(T), dma(T), dma(B * T), dma(B * T),
        ],
        cost_estimate=pl.CostEstimate(flops=flops, bytes_accessed=8 << 20, transcendentals=0),
        compiler_params=pltpu.CompilerParams(
            collective_id=0, has_side_effects=True, vmem_limit_bytes=56 << 20),
    )(hidden[0], target[0], weight[0], gain)
    return merged, merged_gain[0]


def solution(mesh):
    T, Z, X = (mesh.shape[a] for a in ("template", "fsdp", "dp"))
    in_specs = (
        P("template", ("fsdp", "dp"), None),
        P("template", ("fsdp", "dp"), None),
        P("template", "fsdp", None),
        P("template", "fsdp"),
    )
    out_specs = (P(("fsdp", "dp"), None), P(("fsdp", "dp")))
    return jax.shard_map(functools.partial(body, T, Z, X), mesh=mesh, in_specs=in_specs,
                         out_specs=out_specs, check_vma=False)
```

```python
import functools
import math

import jax
import jax.numpy as jnp
from jax import lax
from jax.experimental import pallas as pl
from jax.experimental.pallas import tpu as pltpu
from jax.sharding import PartitionSpec as P

F32 = jnp.float32
BF16 = jnp.bfloat16
MESH = pl.DeviceIdType.MESH


def flip(a, k):
    b = 1
    while b <= k:
        if k & b:
            a = a + b - 2 * b * ((a // b) % 2)
        b *= 2
    return a


def far_first(n):
    return list(range(n // 2, n)) + list(range(1, n // 2))


def kernel(T, Z, X, C, B, h_ref, t_ref, w_ref, g_ref, o_ref, og_ref,
           recv, xbuf, turned, rz, rx, rcol, own, ps, rs, dall, sqt, fsend, frecv,
           f1send, f1recv, wq, gbuf,
           h_ss, h_rs, r_ss, r_rs, x_ss, x_rs, rx_ss, rx_rs, p_ss, p_rs,
           d_ss, d_rs, e_ss, e_rs, w_ss, w_rs, f_ss, f_rs, g_ss, g_rs, o_ss, o_rs):
    m, z, x = (lax.axis_index(a) for a in ("template", "fsdp", "dp"))
    tb, D = h_ref.shape
    FS, H = w_ref.shape
    mine = FS // X
    Q = mine // T
    tc = tb // C
    ZR = Z * tc
    HB = H // B
    tokens = C * X * ZR
    scale = 1.0 / math.sqrt(D)
    pending = []

    def zdev(k):
        return (m, flip(z, k), x)

    def xdev(k):
        return (m, z, flip(x, k))

    def tdev(k):
        return (flip(m, k), z, x)

    def send(src, dst, ss, rs_, dev):
        c = pltpu.make_async_remote_copy(src_ref=src, dst_ref=dst, send_sem=ss, recv_sem=rs_,
                                         device_id=dev, device_id_type=MESH)
        c.start()
        pending.append(c)

    def arrived(dst, sem):
        pltpu.make_async_copy(dst, dst, sem).wait()

    def cols(a, width):
        return pl.ds(pl.multiple_of(a * width, width), width)

    peers = ([zdev(k) for k in range(1, Z)] + [xdev(k) for k in range(1, X)]
             + [tdev(k) for k in range(1, T)])
    barrier = pltpu.get_barrier_semaphore()
    for dev in peers:
        pl.semaphore_signal(barrier, inc=1, device_id=dev, device_id_type=MESH)
    pl.semaphore_wait(barrier, len(peers))

    def send_hidden(c):
        for k in far_first(Z):
            send(h_ref.at[pl.ds(c * tc, tc), cols(flip(z, k), FS)], recv.at[c, k],
                 h_ss.at[c * Z + k], h_rs.at[c * Z + k], zdev(k))

    send_hidden(0)

    step = min(512, D)

    def add_squares(i, acc):
        c = h_ref[:, cols(i, step)].astype(F32)
        c = c * c
        for a in range(0, step, 128):
            acc = acc + c[:, a:a + 128]
        return acc

    acc = lax.fori_loop(0, D // step, add_squares, jnp.zeros((tb, 128), F32))
    ratio = lax.rsqrt(jnp.sum(acc, axis=1, keepdims=True) / D + 1e-05)
    rz[0] = jnp.broadcast_to(ratio, (tb, 128)).T[0:8, :]
    for k in far_first(Z):
        send(rz.at[0], rz.at[k], r_ss.at[k], r_rs.at[k], zdev(k))
    for c in range(1, min(C, 2)):
        send_hidden(c)
    for k in range(1, T):
        send(w_ref.at[cols(x * T + flip(m, k), Q)], wq.at[k], w_ss.at[k], w_rs.at[k], tdev(k))

    def put_column(row_ref, j, k):
        col = jnp.broadcast_to(row_ref[0:1, :], (128, 128)).T
        for c in range(C):
            rcol[c, j, k] = col[c * tc:(c + 1) * tc, :]

    wstep = min(512, FS)

    def partial(c):
        r = rcol[c, 0].reshape(ZR, 128)[:, 0:1]

        def body(i, total):
            here = cols(i, wstep)
            n = (recv[c, :, :, here].reshape(ZR, wstep).astype(F32) * r
                 * g_ref[:, here].astype(F32)).astype(BF16)
            return total + jnp.dot(n, w_ref[here, :], preferred_element_type=F32)

        v = lax.fori_loop(0, FS // wstep, body, jnp.zeros((ZR, H), F32))
        own[pl.ds(c * tc, tc), :] = v[0:tc, :]
        for i in range(B):
            for k in range(1, Z):
                ps[i, k, pl.ds(c * tc, tc), :] = (
                    v[k * tc:(k + 1) * tc, i * HB:(i + 1) * HB].astype(BF16))

    fstep = min(256, mine)

    def squares(c, j):
        r = rcol[c, j].reshape(ZR, 128)[:, 0:1]
        first = (c * X + j) * ZR

        def body(i, _):
            here = cols(i, fstep)
            g = g_ref[:, pl.ds(pl.multiple_of(x * mine + i * fstep, fstep), fstep)].astype(F32)
            n = xbuf[c, j, :, :, here].reshape(ZR, fstep).astype(F32) * r * g
            n = n.astype(BF16).astype(F32)
            sqt[here, first:first + ZR] = (n * n).T.astype(BF16)
            return 0

        lax.fori_loop(0, mine // fstep, body, 0)

    def own_squares(c):
        xbuf[c, 0] = recv[c, :, :, cols(x, mine)]
        squares(c, 0)

    def other_squares(c):
        for j in range(1, X):
            if c == 0:
                arrived(rx.at[j], rx_rs.at[j])
                for k in range(Z):
                    put_column(rx.at[j, k], j, k)
            arrived(xbuf.at[c, j], x_rs.at[c * X + j])
            squares(c, j)

    for c in range(C):
        recv[c, 0] = h_ref[pl.ds(c * tc, tc), cols(z, FS)]
    turned[...] = w_ref[cols(x, mine), :].T
    put_column(rz.at[0], 0, 0)
    for k in range(1, Z):
        arrived(rz.at[k], r_rs.at[k])
        put_column(rz.at[k], 0, k)
    for j in range(1, X):
        send(rz, rx.at[j], rx_ss.at[j], rx_rs.at[j], xdev(j))
    for c in range(C):
        for k in far_first(Z):
            arrived(recv.at[c, k], h_rs.at[c * Z + k])
        if c + 2 < C:
            send_hidden(c + 2)
        for j in range(1, X):
            send(recv.at[c, :, :, cols(flip(x, j), mine)], xbuf.at[c, j],
                 x_ss.at[c * X + j], x_rs.at[c * X + j], xdev(j))
        partial(c)
        if c < C - 1:
            own_squares(c)
            if c:
                other_squares(c - 1)

    def give_partials(i):
        for k in far_first(Z):
            send(ps.at[i, k], rs.at[i, k], p_ss.at[i * Z + k], p_rs.at[i * Z + k], zdev(k))

    def residual(i):
        here = slice(i * HB, (i + 1) * HB)
        v = own[:, here]
        for k in range(1, Z):
            arrived(rs.at[i, k], p_rs.at[i * Z + k])
            v = v + rs[i, k].astype(F32)
        d = (v * scale - t_ref[:, here].astype(F32)).astype(BF16)
        dall[i, :, 0, 0] = d.reshape(C, tc, HB)
        for k in far_first(Z):
            send(dall.at[i, :, 0, 0], dall.at[i, :, 0, k], d_ss.at[i * Z + k], d_rs.at[i * Z + k],
                 zdev(k))
        forward(i, 0)

    def forward(i, k):
        for j in range(1, X):
            s = (i * X + j) * Z + k
            send(dall.at[i, :, 0, k], dall.at[i, :, j, k], e_ss.at[s], e_rs.at[s], xdev(j))

    def residuals_on(i):
        for k in far_first(Z):
            arrived(dall.at[i, :, 0, k], d_rs.at[i * Z + k])
            forward(i, k)

    def fisher_rows(i, q):
        d = dall[i].reshape(tokens, HB).astype(F32)
        return jnp.dot(sqt[cols(q, Q), :], (d * d).astype(BF16), preferred_element_type=F32)

    def fisher(i):
        for j in range(1, X):
            for k in range(Z):
                s = (i * X + j) * Z + k
                arrived(dall.at[i, :, j, k], e_rs.at[s])
        for k in far_first(T):
            f = fisher_rows(i, flip(m, k))
            if k == 1:
                f1send[i] = f
                send(f1send.at[i], f1recv.at[i], f_ss.at[i * T + k], f_rs.at[i * T + k], tdev(k))
            else:
                fsend[i, k] = f.astype(BF16)
                send(fsend.at[i, k], frecv.at[i, k], f_ss.at[i * T + k], f_rs.at[i * T + k],
                     tdev(k))

    def block(j, i):
        return o_ref.at[cols(flip(m, j), Q), pl.ds(i * HB, HB)]

    def share(j, b, i):
        s = i * T + (j ^ b)
        send(block(j, i), block(j, i), o_ss.at[s], o_rs.at[s], tdev(b))

    def merge(i):
        here = slice(i * HB, (i + 1) * HB)
        den = fisher_rows(i, m)
        num = den * w_ref[cols(x * T + m, Q), here].astype(F32)
        for k in range(1, T):
            if i == 0:
                arrived(wq.at[k], w_rs.at[k])
            if k == 1:
                arrived(f1recv.at[i], f_rs.at[i * T + k])
                f = f1recv[i]
            else:
                arrived(frecv.at[i, k], f_rs.at[i * T + k])
                f = frecv[i, k].astype(F32)
            den = den + f
            num = num + f * wq[k, :, here].astype(F32)
        o_ref[cols(m, Q), here] = num / den
        share(0, T // 2, i)

    def share_on(i):
        held, b = [0], T // 2
        while b > 1:
            for j in held:
                arrived(block(j ^ b, i), o_rs.at[i * T + (j ^ b)])
                share(j, b // 2, i)
                share(j ^ b, b // 2, i)
            held = held + [j ^ b for j in held]
            b //= 2

    def back(c, j, total):
        d = jnp.concatenate([dall[i, c, j].reshape(ZR, HB) for i in range(B)], axis=1)
        b = jnp.dot(d, turned[...], preferred_element_type=F32) * scale
        r = rcol[c, j].reshape(ZR, 128)[:, 0:1]
        b = b * (xbuf[c, j].reshape(ZR, mine).astype(F32) * r)
        return total + jnp.sum(b * b, axis=0, keepdims=True)

    give_partials(0)
    if B > 1:
        give_partials(1)
    own_squares(C - 1)
    for t in range(B + 4):
        if t < B:
            residual(t)
        if t + 2 < B:
            give_partials(t + 2)
        if t == 0 and C > 1:
            other_squares(C - 2)
        if 0 <= t - 1 < B:
            residuals_on(t - 1)
        if t == 1:
            other_squares(C - 1)
        if 0 <= t - 2 < B:
            fisher(t - 2)
        if 0 <= t - 3 < B:
            if t - 3 == B - 1:
                gfish = jnp.zeros((1, mine), F32)
                for c in range(C):
                    for j in range(X):
                        gfish = back(c, j, gfish)
                gbuf[0, 0:1, :] = gfish * g_ref[:, cols(x, mine)].astype(F32)
                gbuf[0, 1:2, :] = gfish
                gbuf[0, 2:8, :] = jnp.zeros((6, mine), F32)
                for k in range(1, T):
                    send(gbuf.at[0], gbuf.at[k], g_ss.at[k], g_rs.at[k], tdev(k))
            merge(t - 3)
        if 0 <= t - 4 < B:
            share_on(t - 4)

    for k in range(1, T):
        arrived(gbuf.at[k], g_rs.at[k])
    sums = [gbuf[k] for k in range(T)]
    while len(sums) > 1:
        sums = [sums[i] + sums[i + 1] for i in range(0, len(sums), 2)]
    og_ref[...] = sums[0][0:1, :] / sums[0][1:2, :]
    for i in range(B):
        for j in range(0, T, 2):
            arrived(block(j ^ 1, i), o_rs.at[i * T + (j ^ 1)])
    for c in pending:
        c.wait_send()


def hand_on(i_ref, o_ref):
    o_ref[...] = i_ref[...]


def body(T, Z, X, hidden, target, weight, gain):
    _, tb, D = hidden.shape
    _, FS, H = weight.shape
    mine = FS // X
    Q = mine // T
    S = X * Z
    C = 4
    B = H // 128
    tc = tb // C
    dma = lambda n: pltpu.SemaphoreType.DMA((n,))
    vmem = pltpu.VMEM
    flops = 2 * S * tb * mine * H * 3
    merged, merged_gain = pl.pallas_call(
        functools.partial(kernel, T, Z, X, C, B),
        out_shape=(jax.ShapeDtypeStruct((mine, H), F32), jax.ShapeDtypeStruct((1, mine), F32)),
        in_specs=[pl.BlockSpec(memory_space=pltpu.VMEM)] * 4,
        out_specs=[pl.BlockSpec(memory_space=pltpu.VMEM)] * 2,
        scratch_shapes=[
            vmem((C, Z, tc, FS), BF16),
            vmem((C, X, Z, tc, mine), BF16),
            vmem((H, mine), BF16),
            vmem((Z, 8, 128), F32),
            vmem((X, Z, 8, 128), F32),
            vmem((C, X, Z, tc, 128), F32),
            vmem((tb, H), F32),
            vmem((B, Z, tb, H // B), BF16),
            vmem((B, Z, tb, H // B), BF16),
            vmem((B, C, X, Z, tc, H // B), BF16),
            vmem((mine, S * tb), BF16),
            vmem((B, T, Q, H // B), BF16),
            vmem((B, T, Q, H // B), BF16),
            vmem((B, Q, H // B), F32),
            vmem((B, Q, H // B), F32),
            vmem((T, Q, H), BF16),
            vmem((T, 8, mine), F32),
            dma(C * Z), dma(C * Z), dma(Z), dma(Z), dma(C * X), dma(C * X), dma(X), dma(X),
            dma(B * Z), dma(B * Z), dma(B * Z), dma(B * Z), dma(B * S), dma(B * S),
            dma(T), dma(T), dma(B * T), dma(B * T), dma(T), dma(T), dma(B * T), dma(B * T),
        ],
        cost_estimate=pl.CostEstimate(flops=flops, bytes_accessed=8 << 20, transcendentals=0),
        compiler_params=pltpu.CompilerParams(
            collective_id=0, has_side_effects=True, vmem_limit_bytes=56 << 20),
    )(hidden[0], target[0], weight[0], gain)
    rows = mine // 4
    merged = pl.pallas_call(
        hand_on,
        out_shape=jax.ShapeDtypeStruct((mine, H), F32),
        grid=(4,),
        in_specs=[pl.BlockSpec((rows, H), lambda i: (i, 0))],
        out_specs=pl.BlockSpec((rows, H), lambda i: (i, 0)),
    )(merged)
    return merged, merged_gain[0]


def solution(mesh):
    T, Z, X = (mesh.shape[a] for a in ("template", "fsdp", "dp"))
    in_specs = (
        P("template", ("fsdp", "dp"), None),
        P("template", ("fsdp", "dp"), None),
        P("template", "fsdp", None),
        P("template", "fsdp"),
    )
    out_specs = (P(("fsdp", "dp"), None), P(("fsdp", "dp")))
    return jax.shard_map(functools.partial(body, T, Z, X), mesh=mesh, in_specs=in_specs,
                         out_specs=out_specs, check_vma=False)
```

```python
import functools
import math

import jax
import jax.numpy as jnp
from jax import lax
from jax.experimental import pallas as pl
from jax.experimental.pallas import tpu as pltpu
from jax.sharding import PartitionSpec as P

F32 = jnp.float32
BF16 = jnp.bfloat16
MESH = pl.DeviceIdType.MESH


def flip(a, k):
    b = 1
    while b <= k:
        if k & b:
            a = a + b - 2 * b * ((a // b) % 2)
        b *= 2
    return a


def far_first(n):
    return list(range(n // 2, n)) + list(range(1, n // 2))


def kernel(T, Z, X, C, B, h_ref, t_ref, w_ref, g_ref, o_ref, og_ref,
           recv, xbuf, turned, rz, rx, rcol, pacc, ps, rs, dall, sqt, fsend, frecv,
           f1send, f1recv, wq, gbuf,
           h_ss, h_rs, r_ss, r_rs, x_ss, x_rs, rx_ss, rx_rs, p_ss, p_rs,
           d_ss, d_rs, e_ss, e_rs, w_ss, w_rs, f_ss, f_rs, g_ss, g_rs, o_ss, o_rs):
    m, z, x = (lax.axis_index(a) for a in ("template", "fsdp", "dp"))
    tb, D = h_ref.shape
    FS, H = w_ref.shape
    mine = FS // X
    Q = mine // T
    tc = tb // C
    ZR = Z * tc
    HB = H // B
    tokens = C * X * ZR
    scale = 1.0 / math.sqrt(D)
    pending = []

    def zdev(k):
        return (m, flip(z, k), x)

    def xdev(k):
        return (m, z, flip(x, k))

    def tdev(k):
        return (flip(m, k), z, x)

    def send(src, dst, ss, rs_, dev):
        c = pltpu.make_async_remote_copy(src_ref=src, dst_ref=dst, send_sem=ss, recv_sem=rs_,
                                         device_id=dev, device_id_type=MESH)
        c.start()
        pending.append(c)

    def arrived(dst, sem):
        pltpu.make_async_copy(dst, dst, sem).wait()

    def cols(a, width):
        return pl.ds(pl.multiple_of(a * width, width), width)

    peers = ([zdev(k) for k in range(1, Z)] + [xdev(k) for k in range(1, X)]
             + [tdev(k) for k in range(1, T)])
    barrier = pltpu.get_barrier_semaphore()
    for dev in peers:
        pl.semaphore_signal(barrier, inc=1, device_id=dev, device_id_type=MESH)
    pl.semaphore_wait(barrier, len(peers))

    def send_hidden(c):
        for k in far_first(Z):
            send(h_ref.at[pl.ds(c * tc, tc), cols(flip(z, k), FS)], recv.at[c, k],
                 h_ss.at[c * Z + k], h_rs.at[c * Z + k], zdev(k))

    send_hidden(0)

    step = min(512, D)

    def add_squares(i, acc):
        c = h_ref[:, cols(i, step)].astype(F32)
        c = c * c
        for a in range(0, step, 128):
            acc = acc + c[:, a:a + 128]
        return acc

    acc = lax.fori_loop(0, D // step, add_squares, jnp.zeros((tb, 128), F32))
    ratio = lax.rsqrt(jnp.sum(acc, axis=1, keepdims=True) / D + 1e-05)
    rz[0] = jnp.broadcast_to(ratio, (tb, 128)).T[0:8, :]
    for k in far_first(Z):
        send(rz.at[0], rz.at[k], r_ss.at[k], r_rs.at[k], zdev(k))
    for c in range(1, min(C, 2)):
        send_hidden(c)
    for k in range(1, T):
        send(w_ref.at[cols(x * T + flip(m, k), Q)], wq.at[k], w_ss.at[k], w_rs.at[k], tdev(k))

    def put_column(row_ref, j, k):
        col = jnp.broadcast_to(row_ref[0:1, :], (128, 128)).T
        for c in range(C):
            rcol[c, j, k] = col[c * tc:(c + 1) * tc, :]

    wstep = min(512, FS)

    def partial(c):
        r = rcol[c, 0].reshape(ZR, 128)[:, 0:1]

        def body(i, total):
            here = cols(i, wstep)
            n = (recv[c, :, :, here].reshape(ZR, wstep).astype(F32) * r
                 * g_ref[:, here].astype(F32)).astype(BF16)
            return total + jnp.dot(n, w_ref[here, :], preferred_element_type=F32)

        v = lax.fori_loop(0, FS // wstep, body, jnp.zeros((ZR, H), F32))
        pacc[c] = v.reshape(Z, tc, H)

    steps = Z.bit_length() - 1

    def sum_send(c, n):
        b = 1 << n
        for k in range(b, Z, 2 * b):
            ps[c, k] = pacc[c, k].astype(BF16)
            send(ps.at[c, k], rs.at[c, k], p_ss.at[c * Z + k], p_rs.at[c * Z + k], zdev(b))

    def sum_take(c, n):
        b = 1 << n
        for k in range(b, Z, 2 * b):
            arrived(rs.at[c, k], p_rs.at[c * Z + k])
            pacc[c, k - b] += rs[c, k].astype(F32)

    def sum_on(t):
        for n in range(1, steps + 1):
            if 0 <= t - n < C:
                sum_take(t - n, n - 1)
                if n < steps:
                    sum_send(t - n, n)

    fstep = min(256, mine)

    def squares(c, j):
        r = rcol[c, j].reshape(ZR, 128)[:, 0:1]
        first = (c * X + j) * ZR

        def body(i, _):
            here = cols(i, fstep)
            g = g_ref[:, pl.ds(pl.multiple_of(x * mine + i * fstep, fstep), fstep)].astype(F32)
            n = xbuf[c, j, :, :, here].reshape(ZR, fstep).astype(F32) * r * g
            n = n.astype(BF16).astype(F32)
            sqt[here, first:first + ZR] = (n * n).T.astype(BF16)
            return 0

        lax.fori_loop(0, mine // fstep, body, 0)

    def own_squares(c):
        xbuf[c, 0] = recv[c, :, :, cols(x, mine)]
        squares(c, 0)

    def other_squares(c):
        for j in range(1, X):
            if c == 0:
                arrived(rx.at[j], rx_rs.at[j])
                for k in range(Z):
                    put_column(rx.at[j, k], j, k)
            arrived(xbuf.at[c, j], x_rs.at[c * X + j])
            squares(c, j)

    for c in range(C):
        recv[c, 0] = h_ref[pl.ds(c * tc, tc), cols(z, FS)]
    turned[...] = w_ref[cols(x, mine), :].T
    put_column(rz.at[0], 0, 0)
    for k in range(1, Z):
        arrived(rz.at[k], r_rs.at[k])
        put_column(rz.at[k], 0, k)
    for j in range(1, X):
        send(rz, rx.at[j], rx_ss.at[j], rx_rs.at[j], xdev(j))
    for c in range(C):
        for k in far_first(Z):
            arrived(recv.at[c, k], h_rs.at[c * Z + k])
        if c + 2 < C:
            send_hidden(c + 2)
        for j in range(1, X):
            send(recv.at[c, :, :, cols(flip(x, j), mine)], xbuf.at[c, j],
                 x_ss.at[c * X + j], x_rs.at[c * X + j], xdev(j))
        partial(c)
        sum_send(c, 0)
        sum_on(c)
        own_squares(c)
        if c < C - 1:
            if c:
                other_squares(c - 1)

    def residual(i):
        here = slice(i * HB, (i + 1) * HB)
        v = pacc[:, 0, :, here].reshape(tb, HB)
        d = (v * scale - t_ref[:, here].astype(F32)).astype(BF16)
        dall[i, :, 0, 0] = d.reshape(C, tc, HB)
        for k in far_first(Z):
            send(dall.at[i, :, 0, 0], dall.at[i, :, 0, k], d_ss.at[i * Z + k], d_rs.at[i * Z + k],
                 zdev(k))
        forward(i, 0)

    def forward(i, k):
        for j in range(1, X):
            s = (i * X + j) * Z + k
            send(dall.at[i, :, 0, k], dall.at[i, :, j, k], e_ss.at[s], e_rs.at[s], xdev(j))

    def residuals_on(i):
        for k in far_first(Z):
            arrived(dall.at[i, :, 0, k], d_rs.at[i * Z + k])
            forward(i, k)

    def fisher_rows(i, q):
        d = dall[i].reshape(tokens, HB).astype(F32)
        return jnp.dot(sqt[cols(q, Q), :], (d * d).astype(BF16), preferred_element_type=F32)

    def fisher(i):
        for j in range(1, X):
            for k in range(Z):
                s = (i * X + j) * Z + k
                arrived(dall.at[i, :, j, k], e_rs.at[s])
        for k in far_first(T):
            f = fisher_rows(i, flip(m, k))
            if k == 1:
                f1send[i] = f
                send(f1send.at[i], f1recv.at[i], f_ss.at[i * T + k], f_rs.at[i * T + k], tdev(k))
            else:
                fsend[i, k] = f.astype(BF16)
                send(fsend.at[i, k], frecv.at[i, k], f_ss.at[i * T + k], f_rs.at[i * T + k],
                     tdev(k))

    def block(j, i):
        return o_ref.at[cols(flip(m, j), Q), pl.ds(i * HB, HB)]

    def share(j, b, i):
        s = i * T + (j ^ b)
        send(block(j, i), block(j, i), o_ss.at[s], o_rs.at[s], tdev(b))

    def merge(i):
        here = slice(i * HB, (i + 1) * HB)
        den = fisher_rows(i, m)
        num = den * w_ref[cols(x * T + m, Q), here].astype(F32)
        for k in range(1, T):
            if i == 0:
                arrived(wq.at[k], w_rs.at[k])
            if k == 1:
                arrived(f1recv.at[i], f_rs.at[i * T + k])
                f = f1recv[i]
            else:
                arrived(frecv.at[i, k], f_rs.at[i * T + k])
                f = frecv[i, k].astype(F32)
            den = den + f
            num = num + f * wq[k, :, here].astype(F32)
        o_ref[cols(m, Q), here] = num / den
        share(0, T // 2, i)

    def share_on(i):
        held, b = [0], T // 2
        while b > 1:
            for j in held:
                arrived(block(j ^ b, i), o_rs.at[i * T + (j ^ b)])
                share(j, b // 2, i)
                share(j ^ b, b // 2, i)
            held = held + [j ^ b for j in held]
            b //= 2

    def back(c, j, total):
        d = jnp.concatenate([dall[i, c, j].reshape(ZR, HB) for i in range(B)], axis=1)
        b = jnp.dot(d, turned[...], preferred_element_type=F32) * scale
        r = rcol[c, j].reshape(ZR, 128)[:, 0:1]
        b = b * (xbuf[c, j].reshape(ZR, mine).astype(F32) * r)
        return total + jnp.sum(b * b, axis=0, keepdims=True)

    sum_on(C)
    if C > 1:
        other_squares(C - 2)
    for t in range(C + 1, C + steps):
        sum_on(t)
    for i in range(B):
        residual(i)
    for t in range(B + 3):
        if t < B:
            residuals_on(t)
        if t == 0:
            other_squares(C - 1)
        if 0 <= t - 1 < B:
            fisher(t - 1)
        if 0 <= t - 2 < B:
            if t - 2 == B - 1:
                gfish = jnp.zeros((1, mine), F32)
                for c in range(C):
                    for j in range(X):
                        gfish = back(c, j, gfish)
                gbuf[0, 0:1, :] = gfish * g_ref[:, cols(x, mine)].astype(F32)
                gbuf[0, 1:2, :] = gfish
                gbuf[0, 2:8, :] = jnp.zeros((6, mine), F32)
                for k in range(1, T):
                    send(gbuf.at[0], gbuf.at[k], g_ss.at[k], g_rs.at[k], tdev(k))
            merge(t - 2)
        if 0 <= t - 3 < B:
            share_on(t - 3)

    for k in range(1, T):
        arrived(gbuf.at[k], g_rs.at[k])
    sums = [gbuf[k] for k in range(T)]
    while len(sums) > 1:
        sums = [sums[i] + sums[i + 1] for i in range(0, len(sums), 2)]
    og_ref[...] = sums[0][0:1, :] / sums[0][1:2, :]
    for i in range(B):
        for j in range(0, T, 2):
            arrived(block(j ^ 1, i), o_rs.at[i * T + (j ^ 1)])
    for c in pending:
        c.wait_send()


def hand_on(i_ref, o_ref, sems):
    rows = i_ref.shape[0] // 4
    copies = [pltpu.make_async_copy(i_ref.at[pl.ds(i * rows, rows)], o_ref.at[pl.ds(i * rows, rows)],
                                    sems.at[i]) for i in range(4)]
    for c in copies:
        c.start()
    for c in copies:
        c.wait()


def body(T, Z, X, hidden, target, weight, gain):
    _, tb, D = hidden.shape
    _, FS, H = weight.shape
    mine = FS // X
    Q = mine // T
    S = X * Z
    C = 4
    B = H // 128
    tc = tb // C
    dma = lambda n: pltpu.SemaphoreType.DMA((n,))
    vmem = pltpu.VMEM
    flops = 2 * S * tb * mine * H * 3
    merged, merged_gain = pl.pallas_call(
        functools.partial(kernel, T, Z, X, C, B),
        out_shape=(jax.ShapeDtypeStruct((mine, H), F32), jax.ShapeDtypeStruct((1, mine), F32)),
        in_specs=[pl.BlockSpec(memory_space=pltpu.VMEM)] * 4,
        out_specs=[pl.BlockSpec(memory_space=pltpu.VMEM)] * 2,
        scratch_shapes=[
            vmem((C, Z, tc, FS), BF16),
            vmem((C, X, Z, tc, mine), BF16),
            vmem((H, mine), BF16),
            vmem((Z, 8, 128), F32),
            vmem((X, Z, 8, 128), F32),
            vmem((C, X, Z, tc, 128), F32),
            vmem((C, Z, tc, H), F32),
            vmem((C, Z, tc, H), BF16),
            vmem((C, Z, tc, H), BF16),
            vmem((B, C, X, Z, tc, H // B), BF16),
            vmem((mine, S * tb), BF16),
            vmem((B, T, Q, H // B), BF16),
            vmem((B, T, Q, H // B), BF16),
            vmem((B, Q, H // B), F32),
            vmem((B, Q, H // B), F32),
            vmem((T, Q, H), BF16),
            vmem((T, 8, mine), F32),
            dma(C * Z), dma(C * Z), dma(Z), dma(Z), dma(C * X), dma(C * X), dma(X), dma(X),
            dma(C * Z), dma(C * Z), dma(B * Z), dma(B * Z), dma(B * S), dma(B * S),
            dma(T), dma(T), dma(B * T), dma(B * T), dma(T), dma(T), dma(B * T), dma(B * T),
        ],
        cost_estimate=pl.CostEstimate(flops=flops, bytes_accessed=8 << 20, transcendentals=0),
        compiler_params=pltpu.CompilerParams(
            collective_id=0, has_side_effects=True, vmem_limit_bytes=56 << 20),
    )(hidden[0], target[0], weight[0], gain)
    merged = pl.pallas_call(
        hand_on,
        out_shape=jax.ShapeDtypeStruct((mine, H), F32),
        in_specs=[pl.BlockSpec(memory_space=pl.ANY)],
        out_specs=pl.BlockSpec(memory_space=pl.ANY),
        scratch_shapes=[dma(4)],
    )(merged)
    return merged, merged_gain[0]


def solution(mesh):
    T, Z, X = (mesh.shape[a] for a in ("template", "fsdp", "dp"))
    in_specs = (
        P("template", ("fsdp", "dp"), None),
        P("template", ("fsdp", "dp"), None),
        P("template", "fsdp", None),
        P("template", "fsdp"),
    )
    out_specs = (P(("fsdp", "dp"), None), P(("fsdp", "dp")))
    return jax.shard_map(functools.partial(body, T, Z, X), mesh=mesh, in_specs=in_specs,
                         out_specs=out_specs, check_vma=False)
```

```python
import functools
import math

import jax
import jax.numpy as jnp
from jax import lax
from jax.experimental import pallas as pl
from jax.experimental.pallas import tpu as pltpu
from jax.sharding import PartitionSpec as P

F32 = jnp.float32
BF16 = jnp.bfloat16
MESH = pl.DeviceIdType.MESH


def flip(a, k):
    b = 1
    while b <= k:
        if k & b:
            a = a + b - 2 * b * ((a // b) % 2)
        b *= 2
    return a


def far_first(n):
    return list(range(n // 2, n)) + list(range(1, n // 2))


def kernel(T, Z, X, C, B, h_ref, t_ref, w_ref, g_ref, o_ref, og_ref,
           recv, xbuf, turned, rz, rx, rcol, own, ps, rs, dall, sqt, fsend, frecv,
           f1send, f1recv, wq, gbuf,
           h_ss, h_rs, r_ss, r_rs, x_ss, x_rs, rx_ss, rx_rs, p_ss, p_rs,
           d_ss, d_rs, e_ss, e_rs, w_ss, w_rs, f_ss, f_rs, g_ss, g_rs, o_ss, o_rs):
    m, z, x = (lax.axis_index(a) for a in ("template", "fsdp", "dp"))
    tb, D = h_ref.shape
    FS, H = w_ref.shape
    mine = FS // X
    Q = mine // T
    tc = tb // C
    ZR = Z * tc
    HB = H // B
    tokens = C * X * ZR
    scale = 1.0 / math.sqrt(D)
    pending = []

    def zdev(k):
        return (m, flip(z, k), x)

    def xdev(k):
        return (m, z, flip(x, k))

    def tdev(k):
        return (flip(m, k), z, x)

    def send(src, dst, ss, rs_, dev):
        c = pltpu.make_async_remote_copy(src_ref=src, dst_ref=dst, send_sem=ss, recv_sem=rs_,
                                         device_id=dev, device_id_type=MESH)
        c.start()
        pending.append(c)

    def arrived(dst, sem):
        pltpu.make_async_copy(dst, dst, sem).wait()

    def cols(a, width):
        return pl.ds(pl.multiple_of(a * width, width), width)

    peers = ([zdev(k) for k in range(1, Z)] + [xdev(k) for k in range(1, X)]
             + [tdev(k) for k in range(1, T)])
    barrier = pltpu.get_barrier_semaphore()
    for dev in peers:
        pl.semaphore_signal(barrier, inc=1, device_id=dev, device_id_type=MESH)
    pl.semaphore_wait(barrier, len(peers))

    def send_hidden(c):
        for k in far_first(Z):
            send(h_ref.at[pl.ds(c * tc, tc), cols(flip(z, k), FS)], recv.at[c, k],
                 h_ss.at[c * Z + k], h_rs.at[c * Z + k], zdev(k))

    send_hidden(0)

    step = min(512, D)

    def add_squares(i, acc):
        c = h_ref[:, cols(i, step)].astype(F32)
        c = c * c
        for a in range(0, step, 128):
            acc = acc + c[:, a:a + 128]
        return acc

    acc = lax.fori_loop(0, D // step, add_squares, jnp.zeros((tb, 128), F32))
    ratio = lax.rsqrt(jnp.sum(acc, axis=1, keepdims=True) / D + 1e-05)
    rz[0] = jnp.broadcast_to(ratio, (tb, 128)).T[0:8, :]
    for k in far_first(Z):
        send(rz.at[0], rz.at[k], r_ss.at[k], r_rs.at[k], zdev(k))
    for c in range(1, min(C, 2)):
        send_hidden(c)
    for k in range(1, T):
        send(w_ref.at[cols(x * T + flip(m, k), Q)], wq.at[k], w_ss.at[k], w_rs.at[k], tdev(k))

    def put_column(row_ref, j, k):
        col = jnp.broadcast_to(row_ref[0:1, :], (128, 128)).T
        for c in range(C):
            rcol[c, j, k] = col[c * tc:(c + 1) * tc, :]

    wstep = min(512, FS)

    def partial(c):
        r = rcol[c, 0].reshape(ZR, 128)[:, 0:1]

        def body(i, total):
            here = cols(i, wstep)
            n = (recv[c, :, :, here].reshape(ZR, wstep).astype(F32) * r
                 * g_ref[:, here].astype(F32)).astype(BF16)
            return total + jnp.dot(n, w_ref[here, :], preferred_element_type=F32)

        v = lax.fori_loop(0, FS // wstep, body, jnp.zeros((ZR, H), F32))
        own[pl.ds(c * tc, tc), :] = v[0:tc, :]
        for i in range(B):
            for k in range(1, Z):
                ps[i, k, pl.ds(c * tc, tc), :] = (
                    v[k * tc:(k + 1) * tc, i * HB:(i + 1) * HB].astype(BF16))

    fstep = min(256, mine)

    def squares(c, j):
        r = rcol[c, j].reshape(ZR, 128)[:, 0:1]
        first = (c * X + j) * ZR

        def body(i, _):
            here = cols(i, fstep)
            g = g_ref[:, pl.ds(pl.multiple_of(x * mine + i * fstep, fstep), fstep)].astype(F32)
            n = xbuf[c, j, :, :, here].reshape(ZR, fstep).astype(F32) * r * g
            n = n.astype(BF16).astype(F32)
            sqt[here, first:first + ZR] = (n * n).T.astype(BF16)
            return 0

        lax.fori_loop(0, mine // fstep, body, 0)

    def own_squares(c):
        xbuf[c, 0] = recv[c, :, :, cols(x, mine)]
        squares(c, 0)

    def other_squares(c):
        for j in range(1, X):
            if c == 0:
                arrived(rx.at[j], rx_rs.at[j])
                for k in range(Z):
                    put_column(rx.at[j, k], j, k)
            arrived(xbuf.at[c, j], x_rs.at[c * X + j])
            squares(c, j)

    for c in range(C):
        recv[c, 0] = h_ref[pl.ds(c * tc, tc), cols(z, FS)]
    turned[...] = w_ref[cols(x, mine), :].T
    put_column(rz.at[0], 0, 0)
    for k in range(1, Z):
        arrived(rz.at[k], r_rs.at[k])
        put_column(rz.at[k], 0, k)
    for j in range(1, X):
        send(rz, rx.at[j], rx_ss.at[j], rx_rs.at[j], xdev(j))
    for c in range(C):
        for k in far_first(Z):
            arrived(recv.at[c, k], h_rs.at[c * Z + k])
        if c + 2 < C:
            send_hidden(c + 2)
        for j in range(1, X):
            send(recv.at[c, :, :, cols(flip(x, j), mine)], xbuf.at[c, j],
                 x_ss.at[c * X + j], x_rs.at[c * X + j], xdev(j))
        partial(c)
        if c < C - 1:
            own_squares(c)
            if c:
                other_squares(c - 1)

    def give_partials(i):
        for k in far_first(Z):
            send(ps.at[i, k], rs.at[i, k], p_ss.at[i * Z + k], p_rs.at[i * Z + k], zdev(k))

    def residual(i):
        here = slice(i * HB, (i + 1) * HB)
        v = own[:, here]
        for k in range(1, Z):
            arrived(rs.at[i, k], p_rs.at[i * Z + k])
            v = v + rs[i, k].astype(F32)
        d = (v * scale - t_ref[:, here].astype(F32)).astype(BF16)
        dall[i, :, 0, 0] = d.reshape(C, tc, HB)
        for k in far_first(Z):
            send(dall.at[i, :, 0, 0], dall.at[i, :, 0, k], d_ss.at[i * Z + k], d_rs.at[i * Z + k],
                 zdev(k))
        forward(i, 0)

    def forward(i, k):
        for j in range(1, X):
            s = (i * X + j) * Z + k
            send(dall.at[i, :, 0, k], dall.at[i, :, j, k], e_ss.at[s], e_rs.at[s], xdev(j))

    def residuals_on(i):
        for k in far_first(Z):
            arrived(dall.at[i, :, 0, k], d_rs.at[i * Z + k])
            forward(i, k)

    def fisher_rows(i, q):
        d = dall[i].reshape(tokens, HB).astype(F32)
        return jnp.dot(sqt[cols(q, Q), :], (d * d).astype(BF16), preferred_element_type=F32)

    def fisher(i):
        for j in range(1, X):
            for k in range(Z):
                s = (i * X + j) * Z + k
                arrived(dall.at[i, :, j, k], e_rs.at[s])
        for k in far_first(T):
            f = fisher_rows(i, flip(m, k))
            if k == 1:
                f1send[i] = f
                send(f1send.at[i], f1recv.at[i], f_ss.at[i * T + k], f_rs.at[i * T + k], tdev(k))
            else:
                fsend[i, k] = (f * f).astype(BF16)
                send(fsend.at[i, k], frecv.at[i, k], f_ss.at[i * T + k], f_rs.at[i * T + k],
                     tdev(k))

    def block(j, i):
        return o_ref.at[cols(flip(m, j), Q), pl.ds(i * HB, HB)]

    def share(j, b, i):
        s = i * T + (j ^ b)
        send(block(j, i), block(j, i), o_ss.at[s], o_rs.at[s], tdev(b))

    def merge(i):
        here = slice(i * HB, (i + 1) * HB)
        den = fisher_rows(i, m)
        num = den * w_ref[cols(x * T + m, Q), here].astype(F32)
        for k in range(1, T):
            if i == 0:
                arrived(wq.at[k], w_rs.at[k])
            if k == 1:
                arrived(f1recv.at[i], f_rs.at[i * T + k])
                f = f1recv[i]
            else:
                arrived(frecv.at[i, k], f_rs.at[i * T + k])
                f = jnp.sqrt(frecv[i, k].astype(F32))
            den = den + f
            num = num + f * wq[k, :, here].astype(F32)
        v = num / den
        v2 = v * v
        v4 = v2 * v2
        o_ref[cols(m, Q), here] = jnp.where(v < 0, -v4, v4).astype(BF16)
        share(0, T // 2, i)

    def share_on(i):
        held, b = [0], T // 2
        while b > 1:
            for j in held:
                arrived(block(j ^ b, i), o_rs.at[i * T + (j ^ b)])
                share(j, b // 2, i)
                share(j ^ b, b // 2, i)
            held = held + [j ^ b for j in held]
            b //= 2

    def back(c, j, total):
        d = jnp.concatenate([dall[i, c, j].reshape(ZR, HB) for i in range(B)], axis=1)
        b = jnp.dot(d, turned[...], preferred_element_type=F32) * scale
        r = rcol[c, j].reshape(ZR, 128)[:, 0:1]
        b = b * (xbuf[c, j].reshape(ZR, mine).astype(F32) * r)
        return total + jnp.sum(b * b, axis=0, keepdims=True)

    give_partials(0)
    if B > 1:
        give_partials(1)
    own_squares(C - 1)
    for t in range(B + 4):
        if t < B:
            residual(t)
        if t + 2 < B:
            give_partials(t + 2)
        if t == 0 and C > 1:
            other_squares(C - 2)
        if 0 <= t - 1 < B:
            residuals_on(t - 1)
        if t == 1:
            other_squares(C - 1)
        if 0 <= t - 2 < B:
            fisher(t - 2)
        if 0 <= t - 3 < B:
            if t - 3 == B - 1:
                gfish = jnp.zeros((1, mine), F32)
                for c in range(C):
                    for j in range(X):
                        gfish = back(c, j, gfish)
                gbuf[0, 0:1, :] = gfish * g_ref[:, cols(x, mine)].astype(F32)
                gbuf[0, 1:2, :] = gfish
                gbuf[0, 2:8, :] = jnp.zeros((6, mine), F32)
                for k in range(1, T):
                    send(gbuf.at[0], gbuf.at[k], g_ss.at[k], g_rs.at[k], tdev(k))
            merge(t - 3)
        if 0 <= t - 4 < B:
            share_on(t - 4)

    for k in range(1, T):
        arrived(gbuf.at[k], g_rs.at[k])
    sums = [gbuf[k] for k in range(T)]
    while len(sums) > 1:
        sums = [sums[i] + sums[i + 1] for i in range(0, len(sums), 2)]
    og_ref[...] = sums[0][0:1, :] / sums[0][1:2, :]
    for i in range(B):
        for j in range(0, T, 2):
            arrived(block(j ^ 1, i), o_rs.at[i * T + (j ^ 1)])
    for c in pending:
        c.wait_send()


def body(T, Z, X, hidden, target, weight, gain):
    _, tb, D = hidden.shape
    _, FS, H = weight.shape
    mine = FS // X
    Q = mine // T
    S = X * Z
    C = 4
    B = H // 128
    tc = tb // C
    dma = lambda n: pltpu.SemaphoreType.DMA((n,))
    vmem = pltpu.VMEM
    flops = 2 * S * tb * mine * H * 3
    merged, merged_gain = pl.pallas_call(
        functools.partial(kernel, T, Z, X, C, B),
        out_shape=(jax.ShapeDtypeStruct((mine, H), BF16), jax.ShapeDtypeStruct((1, mine), F32)),
        in_specs=[pl.BlockSpec(memory_space=pltpu.VMEM)] * 4,
        out_specs=[pl.BlockSpec(memory_space=pltpu.VMEM)] * 2,
        scratch_shapes=[
            vmem((C, Z, tc, FS), BF16),
            vmem((C, X, Z, tc, mine), BF16),
            vmem((H, mine), BF16),
            vmem((Z, 8, 128), F32),
            vmem((X, Z, 8, 128), F32),
            vmem((C, X, Z, tc, 128), F32),
            vmem((tb, H), F32),
            vmem((B, Z, tb, H // B), BF16),
            vmem((B, Z, tb, H // B), BF16),
            vmem((B, C, X, Z, tc, H // B), BF16),
            vmem((mine, S * tb), BF16),
            vmem((B, T, Q, H // B), BF16),
            vmem((B, T, Q, H // B), BF16),
            vmem((B, Q, H // B), F32),
            vmem((B, Q, H // B), F32),
            vmem((T, Q, H), BF16),
            vmem((T, 8, mine), F32),
            dma(C * Z), dma(C * Z), dma(Z), dma(Z), dma(C * X), dma(C * X), dma(X), dma(X),
            dma(B * Z), dma(B * Z), dma(B * Z), dma(B * Z), dma(B * S), dma(B * S),
            dma(T), dma(T), dma(B * T), dma(B * T), dma(T), dma(T), dma(B * T), dma(B * T),
        ],
        cost_estimate=pl.CostEstimate(flops=flops, bytes_accessed=8 << 20, transcendentals=0),
        compiler_params=pltpu.CompilerParams(
            collective_id=0, has_side_effects=True, vmem_limit_bytes=56 << 20),
    )(hidden[0], target[0], weight[0], gain)
    y = merged.astype(F32)
    r = jnp.sqrt(jnp.sqrt(jnp.abs(y)))
    return jnp.where(y < 0, -r, r), merged_gain[0]


def solution(mesh):
    T, Z, X = (mesh.shape[a] for a in ("template", "fsdp", "dp"))
    in_specs = (
        P("template", ("fsdp", "dp"), None),
        P("template", ("fsdp", "dp"), None),
        P("template", "fsdp", None),
        P("template", "fsdp"),
    )
    out_specs = (P(("fsdp", "dp"), None), P(("fsdp", "dp")))
    return jax.shard_map(functools.partial(body, T, Z, X), mesh=mesh, in_specs=in_specs,
                         out_specs=out_specs, check_vma=False)
```

```python
import functools
import math

import jax
import jax.numpy as jnp
from jax import lax
from jax.experimental import pallas as pl
from jax.experimental.pallas import tpu as pltpu
from jax.sharding import PartitionSpec as P

F32 = jnp.float32
BF16 = jnp.bfloat16
MESH = pl.DeviceIdType.MESH


def flip(a, k):
    b = 1
    while b <= k:
        if k & b:
            a = a + b - 2 * b * ((a // b) % 2)
        b *= 2
    return a


def far_first(n):
    return list(range(n // 2, n)) + list(range(1, n // 2))


def kernel(T, Z, X, C, B, h_ref, t_ref, w_ref, g_ref, o_ref, og_ref,
           recv, xbuf, turned, rz, rx, rcol, own, ps, rs, dall, sqt, fsend, frecv,
           f1send, f1recv, wq, gbuf,
           h_ss, h_rs, r_ss, r_rs, x_ss, x_rs, rx_ss, rx_rs, p_ss, p_rs,
           d_ss, d_rs, e_ss, e_rs, w_ss, w_rs, f_ss, f_rs, g_ss, g_rs, o_ss, o_rs):
    m, z, x = (lax.axis_index(a) for a in ("template", "fsdp", "dp"))
    tb, D = h_ref.shape
    FS, H = w_ref.shape
    mine = FS // X
    Q = mine // T
    tc = tb // C
    ZR = Z * tc
    HB = H // B
    tokens = C * X * ZR
    scale = 1.0 / math.sqrt(D)
    pending = []

    def zdev(k):
        return (m, flip(z, k), x)

    def xdev(k):
        return (m, z, flip(x, k))

    def tdev(k):
        return (flip(m, k), z, x)

    def send(src, dst, ss, rs_, dev):
        c = pltpu.make_async_remote_copy(src_ref=src, dst_ref=dst, send_sem=ss, recv_sem=rs_,
                                         device_id=dev, device_id_type=MESH)
        c.start()
        pending.append(c)

    def arrived(dst, sem):
        pltpu.make_async_copy(dst, dst, sem).wait()

    def cols(a, width):
        return pl.ds(pl.multiple_of(a * width, width), width)

    peers = ([zdev(k) for k in range(1, Z)] + [xdev(k) for k in range(1, X)]
             + [tdev(k) for k in range(1, T)])
    barrier = pltpu.get_barrier_semaphore()
    for dev in peers:
        pl.semaphore_signal(barrier, inc=1, device_id=dev, device_id_type=MESH)
    pl.semaphore_wait(barrier, len(peers))

    def send_hidden(c):
        for k in far_first(Z):
            send(h_ref.at[pl.ds(c * tc, tc), cols(flip(z, k), FS)], recv.at[c, k],
                 h_ss.at[c * Z + k], h_rs.at[c * Z + k], zdev(k))

    send_hidden(0)

    step = min(512, D)

    def add_squares(i, acc):
        c = h_ref[:, cols(i, step)].astype(F32)
        c = c * c
        for a in range(0, step, 128):
            acc = acc + c[:, a:a + 128]
        return acc

    acc = lax.fori_loop(0, D // step, add_squares, jnp.zeros((tb, 128), F32))
    ratio = lax.rsqrt(jnp.sum(acc, axis=1, keepdims=True) / D + 1e-05)
    rz[0] = jnp.broadcast_to(ratio, (tb, 128)).T[0:8, :]
    for k in far_first(Z):
        send(rz.at[0], rz.at[k], r_ss.at[k], r_rs.at[k], zdev(k))
    for c in range(1, min(C, 2)):
        send_hidden(c)
    for k in range(1, T):
        send(w_ref.at[cols(x * T + flip(m, k), Q)], wq.at[k], w_ss.at[k], w_rs.at[k], tdev(k))

    def put_column(row_ref, j, k):
        col = jnp.broadcast_to(row_ref[0:1, :], (128, 128)).T
        for c in range(C):
            rcol[c, j, k] = col[c * tc:(c + 1) * tc, :]

    wstep = min(512, FS)

    def partial(c):
        r = rcol[c, 0].reshape(ZR, 128)[:, 0:1]

        def body(i, total):
            here = cols(i, wstep)
            n = (recv[c, :, :, here].reshape(ZR, wstep).astype(F32) * r
                 * g_ref[:, here].astype(F32)).astype(BF16)
            return total + jnp.dot(n, w_ref[here, :], preferred_element_type=F32)

        v = lax.fori_loop(0, FS // wstep, body, jnp.zeros((ZR, H), F32))
        own[pl.ds(c * tc, tc), :] = v[0:tc, :]
        for i in range(B):
            for k in range(1, Z):
                ps[i, k, pl.ds(c * tc, tc), :] = (
                    v[k * tc:(k + 1) * tc, i * HB:(i + 1) * HB].astype(BF16))

    fstep = min(256, mine)

    def squares(c, j):
        r = rcol[c, j].reshape(ZR, 128)[:, 0:1]
        first = (c * X + j) * ZR

        def body(i, _):
            here = cols(i, fstep)
            g = g_ref[:, pl.ds(pl.multiple_of(x * mine + i * fstep, fstep), fstep)].astype(F32)
            n = xbuf[c, j, :, :, here].reshape(ZR, fstep).astype(F32) * r * g
            n = n.astype(BF16).astype(F32)
            sqt[here, first:first + ZR] = (n * n).T.astype(BF16)
            return 0

        lax.fori_loop(0, mine // fstep, body, 0)

    def own_squares(c):
        xbuf[c, 0] = recv[c, :, :, cols(x, mine)]
        squares(c, 0)

    def other_squares(c):
        for j in range(1, X):
            if c == 0:
                arrived(rx.at[j], rx_rs.at[j])
                for k in range(Z):
                    put_column(rx.at[j, k], j, k)
            arrived(xbuf.at[c, j], x_rs.at[c * X + j])
            squares(c, j)

    for c in range(C):
        recv[c, 0] = h_ref[pl.ds(c * tc, tc), cols(z, FS)]
    turned[...] = w_ref[cols(x, mine), :].T
    put_column(rz.at[0], 0, 0)
    for k in range(1, Z):
        arrived(rz.at[k], r_rs.at[k])
        put_column(rz.at[k], 0, k)
    for j in range(1, X):
        send(rz, rx.at[j], rx_ss.at[j], rx_rs.at[j], xdev(j))
    for c in range(C):
        for k in far_first(Z):
            arrived(recv.at[c, k], h_rs.at[c * Z + k])
        if c + 2 < C:
            send_hidden(c + 2)
        for j in range(1, X):
            send(recv.at[c, :, :, cols(flip(x, j), mine)], xbuf.at[c, j],
                 x_ss.at[c * X + j], x_rs.at[c * X + j], xdev(j))
        partial(c)
        if c < C - 1:
            own_squares(c)
            if c:
                other_squares(c - 1)

    def give_partials(i):
        for k in far_first(Z):
            send(ps.at[i, k], rs.at[i, k], p_ss.at[i * Z + k], p_rs.at[i * Z + k], zdev(k))

    def residual(i):
        here = slice(i * HB, (i + 1) * HB)
        v = own[:, here]
        for k in range(1, Z):
            arrived(rs.at[i, k], p_rs.at[i * Z + k])
            v = v + rs[i, k].astype(F32)
        d = (v * scale - t_ref[:, here].astype(F32)).astype(BF16)
        dall[i, :, 0, 0] = d.reshape(C, tc, HB)
        for k in far_first(Z):
            send(dall.at[i, :, 0, 0], dall.at[i, :, 0, k], d_ss.at[i * Z + k], d_rs.at[i * Z + k],
                 zdev(k))
        forward(i, 0)

    def forward(i, k):
        for j in range(1, X):
            s = (i * X + j) * Z + k
            send(dall.at[i, :, 0, k], dall.at[i, :, j, k], e_ss.at[s], e_rs.at[s], xdev(j))

    def residuals_on(i):
        for k in far_first(Z):
            arrived(dall.at[i, :, 0, k], d_rs.at[i * Z + k])
            forward(i, k)

    def fisher_rows(i, q):
        d = dall[i].reshape(tokens, HB).astype(F32)
        return jnp.dot(sqt[cols(q, Q), :], (d * d).astype(BF16), preferred_element_type=F32)

    def fisher(i):
        for j in range(1, X):
            for k in range(Z):
                s = (i * X + j) * Z + k
                arrived(dall.at[i, :, j, k], e_rs.at[s])
        for k in far_first(T):
            f = fisher_rows(i, flip(m, k))
            if k == 1:
                f1send[i] = f
                send(f1send.at[i], f1recv.at[i], f_ss.at[i * T + k], f_rs.at[i * T + k], tdev(k))
            else:
                fsend[i, k] = (f * f).astype(BF16)
                send(fsend.at[i, k], frecv.at[i, k], f_ss.at[i * T + k], f_rs.at[i * T + k],
                     tdev(k))

    def block(j, i):
        return o_ref.at[cols(flip(m, j), Q), pl.ds(i * HB, HB)]

    def share(j, b, i):
        s = i * T + (j ^ b)
        send(block(j, i), block(j, i), o_ss.at[s], o_rs.at[s], tdev(b))

    def merge(i):
        here = slice(i * HB, (i + 1) * HB)
        den = fisher_rows(i, m)
        num = den * w_ref[cols(x * T + m, Q), here].astype(F32)
        for k in range(1, T):
            if i == 0:
                arrived(wq.at[k], w_rs.at[k])
            if k == 1:
                arrived(f1recv.at[i], f_rs.at[i * T + k])
                f = f1recv[i]
            else:
                arrived(frecv.at[i, k], f_rs.at[i * T + k])
                f = jnp.sqrt(frecv[i, k].astype(F32))
            den = den + f
            num = num + f * wq[k, :, here].astype(F32)
        v = num / den
        v2 = v * v
        v4 = v2 * v2
        o_ref[cols(m, Q), here] = jnp.where(v < 0, -v4, v4).astype(BF16)
        share(0, T // 2, i)

    def share_on(i):
        held, b = [0], T // 2
        while b > 1:
            for j in held:
                arrived(block(j ^ b, i), o_rs.at[i * T + (j ^ b)])
                share(j, b // 2, i)
                share(j ^ b, b // 2, i)
            held = held + [j ^ b for j in held]
            b //= 2

    def back(c, j, total):
        d = jnp.concatenate([dall[i, c, j].reshape(ZR, HB) for i in range(B)], axis=1)
        b = jnp.dot(d, turned[...], preferred_element_type=F32) * scale
        r = rcol[c, j].reshape(ZR, 128)[:, 0:1]
        b = b * (xbuf[c, j].reshape(ZR, mine).astype(F32) * r)
        return total + jnp.sum(b * b, axis=0, keepdims=True)

    give_partials(0)
    if B > 1:
        give_partials(1)
    own_squares(C - 1)
    for t in range(B + 4):
        if t < B:
            residual(t)
        if t + 2 < B:
            give_partials(t + 2)
        if t == 0 and C > 1:
            other_squares(C - 2)
        if 0 <= t - 1 < B:
            residuals_on(t - 1)
        if t == 1:
            other_squares(C - 1)
        if 0 <= t - 2 < B:
            fisher(t - 2)
        if 0 <= t - 3 < B:
            if t - 3 == B - 1:
                gfish = jnp.zeros((1, mine), F32)
                for c in range(C):
                    for j in range(X):
                        gfish = back(c, j, gfish)
                gbuf[0, 0:1, :] = gfish * g_ref[:, cols(x, mine)].astype(F32)
                gbuf[0, 1:2, :] = gfish
                gbuf[0, 2:8, :] = jnp.zeros((6, mine), F32)
                for k in range(1, T):
                    send(gbuf.at[0], gbuf.at[k], g_ss.at[k], g_rs.at[k], tdev(k))
            merge(t - 3)
        if 0 <= t - 4 < B:
            share_on(t - 4)

    for k in range(1, T):
        arrived(gbuf.at[k], g_rs.at[k])
    sums = [gbuf[k] for k in range(T)]
    while len(sums) > 1:
        sums = [sums[i] + sums[i + 1] for i in range(0, len(sums), 2)]
    og_ref[...] = sums[0][0:1, :] / sums[0][1:2, :]
    for i in range(B):
        for j in range(0, T, 2):
            arrived(block(j ^ 1, i), o_rs.at[i * T + (j ^ 1)])
    for c in pending:
        c.wait_send()


def body(T, Z, X, hidden, target, weight, gain):
    _, tb, D = hidden.shape
    _, FS, H = weight.shape
    mine = FS // X
    Q = mine // T
    S = X * Z
    C = 4
    B = H // 256
    tc = tb // C
    dma = lambda n: pltpu.SemaphoreType.DMA((n,))
    vmem = pltpu.VMEM
    flops = 2 * S * tb * mine * H * 3
    merged, merged_gain = pl.pallas_call(
        functools.partial(kernel, T, Z, X, C, B),
        out_shape=(jax.ShapeDtypeStruct((mine, H), BF16), jax.ShapeDtypeStruct((1, mine), F32)),
        in_specs=[pl.BlockSpec(memory_space=pltpu.VMEM)] * 4,
        out_specs=[pl.BlockSpec(memory_space=pltpu.VMEM)] * 2,
        scratch_shapes=[
            vmem((C, Z, tc, FS), BF16),
            vmem((C, X, Z, tc, mine), BF16),
            vmem((H, mine), BF16),
            vmem((Z, 8, 128), F32),
            vmem((X, Z, 8, 128), F32),
            vmem((C, X, Z, tc, 128), F32),
            vmem((tb, H), F32),
            vmem((B, Z, tb, H // B), BF16),
            vmem((B, Z, tb, H // B), BF16),
            vmem((B, C, X, Z, tc, H // B), BF16),
            vmem((mine, S * tb), BF16),
            vmem((B, T, Q, H // B), BF16),
            vmem((B, T, Q, H // B), BF16),
            vmem((B, Q, H // B), F32),
            vmem((B, Q, H // B), F32),
            vmem((T, Q, H), BF16),
            vmem((T, 8, mine), F32),
            dma(C * Z), dma(C * Z), dma(Z), dma(Z), dma(C * X), dma(C * X), dma(X), dma(X),
            dma(B * Z), dma(B * Z), dma(B * Z), dma(B * Z), dma(B * S), dma(B * S),
            dma(T), dma(T), dma(B * T), dma(B * T), dma(T), dma(T), dma(B * T), dma(B * T),
        ],
        cost_estimate=pl.CostEstimate(flops=flops, bytes_accessed=8 << 20, transcendentals=0),
        compiler_params=pltpu.CompilerParams(
            collective_id=0, has_side_effects=True, vmem_limit_bytes=56 << 20),
    )(hidden[0], target[0], weight[0], gain)
    y = merged.astype(F32)
    r = jnp.sqrt(jnp.sqrt(jnp.abs(y)))
    return jnp.where(y < 0, -r, r), merged_gain[0]


def solution(mesh):
    T, Z, X = (mesh.shape[a] for a in ("template", "fsdp", "dp"))
    in_specs = (
        P("template", ("fsdp", "dp"), None),
        P("template", ("fsdp", "dp"), None),
        P("template", "fsdp", None),
        P("template", "fsdp"),
    )
    out_specs = (P(("fsdp", "dp"), None), P(("fsdp", "dp")))
    return jax.shard_map(functools.partial(body, T, Z, X), mesh=mesh, in_specs=in_specs,
                         out_specs=out_specs, check_vma=False)
```
